512 devices in a mesh: region: 16 (over y, core), sub: 32 (over x, z).
Axes of the slice: x: 4, y: 8, z: 8, core: 2. Of those that a mesh axis runs over, the one named last changes fastest.
Arguments:
- feat: bfloat16 [65536, 1024], P(('region', 'sub')), may hold values from -6 to 6
- cotangent: bfloat16 [65536, 1024], P(('region', 'sub')), may hold values from -6 to 6
- weight: bfloat16 [1024, 1024], P('sub'), may hold values from -0.1875 to 0.1875
- nbr_index: int32 [65536, 16], P(('region', 'sub')), may hold values from 0 to 1151, as said below
- degree: int32 [65536], P(('region', 'sub')), may hold values from 1 to 16
- send_rows: int32 [262144, 1], P(('region', 'sub')), may hold values from 0 to 127
- hub_rows: int32 [512], P(('region', 'sub')), may hold values from 0 to 127
Outputs:
- output: bfloat16 [65536, 1024], P(('region', 'sub'))
- grad_feat: bfloat16 [65536, 1024], P(('region', 'sub'))
The draws below stay inside these ranges and needn't reach their ends.
Inputs may be any that keep to these rules, and one draw needn't show every extreme that they name: `nbr_index`: slots k >= degree[t] are padding and carry no edge.
All inputs are finite; a program needn't handle non-finite values.
Results may differ from the reference program's by a relative error of at most 0.0052.
Values may be sent and summed in bfloat16 or wider, within the bound.
A program may use at most 64 MiB of HBM per device.

```python
import jax
import jax.numpy as jnp
from jax import lax

D = 1024
NODE_DEV = 128
NBRS = 16
BOUND = 1
HUB_DEV = 1
NODES = 65536
HUBS = 512
TABLE = 1152
N_REGION = 16
N_SUB = 32
DEVICES = 512


def draw_nbr_index(key, part):
    key = jax.random.fold_in(key, 11)
    kinds_key, local_key, bound_key, hub_key = jax.random.split(key, 4)
    grid_shape = (NODES, NBRS)
    category = jax.random.randint(kinds_key, grid_shape, 0, 20)
    local_pick = jax.random.randint(local_key, grid_shape, 0, NODE_DEV)
    bound_pick = NODE_DEV + jax.random.randint(bound_key, grid_shape, 0, TABLE - NODE_DEV - HUBS)
    hub_pick = TABLE - HUBS + jax.random.randint(hub_key, grid_shape, 0, HUBS)
    picked = jnp.where(category < 12, local_pick, jnp.where(category < 17, bound_pick, hub_pick))
    picked = picked.at[0, NBRS - 1].set(TABLE - 1).at[1, NBRS - 1].set(0)
    return picked.astype(jnp.int32)


def draw_degree(key, part):
    key = jax.random.fold_in(key, 23)
    counts = jax.random.randint(key, (NODES,), 1, NBRS + 1)
    return counts.at[0].set(NBRS).at[1].set(1).astype(jnp.int32)


def with_ends(result, rng, least, high):
    spot = [jax.random.randint(jax.random.fold_in(rng, axis), (), 0, length) for axis, length in enumerate(result.shape)]
    main_axis = result.shape.index(max(result.shape))
    neighbour = spot[:main_axis] + [(spot[main_axis] + 1) % result.shape[main_axis]] + spot[main_axis + 1:]
    return result.at[tuple(spot)].set(least).at[tuple(neighbour)].set(high)


def block_levels(rng, shape, cuts, low, high):
    gain, own = 1.0, jax.random.fold_in(rng, 6)
    for dim, shards_of in cuts:
        draws = jnp.exp(jax.random.uniform(jax.random.fold_in(own, dim), (shards_of,), jnp.float32, low / len(cuts), high / len(cuts)))
        gain = gain * jnp.repeat(draws, shape[dim] // shards_of).reshape([-1 if axis == dim else 1 for axis in range(len(shape))])
    return gain


def normal_values(key, shape, deviation, reach, cuts=(), kind=jnp.bfloat16):
    level = block_levels(key, shape, cuts, -0.22, 0.18) if cuts else 1.0
    result = jax.random.normal(key, shape, jnp.float32) * deviation * level
    return jnp.minimum(jnp.maximum(result, -reach), reach).astype(kind)


def setup_inputs(seed: int = 0) -> dict:
    arg_keys = jax.random.split(jax.random.key(seed), 8)
    feat = normal_values(arg_keys[0], (NODES, D), 1.0, 6.0, ((0, 512),))
    cotangent = normal_values(arg_keys[1], (NODES, D), 1.0, 6.0, ((0, 512),))
    weight = normal_values(arg_keys[2], (D, D), D ** -0.5, 0.1875, ((0, 32),))
    nbr_index = draw_nbr_index(jax.random.fold_in(arg_keys[7], 71), 0)
    degree = draw_degree(jax.random.fold_in(arg_keys[7], 71), 0)
    send_rows = with_ends(jax.random.randint(arg_keys[5], (DEVICES * DEVICES, BOUND), 0, NODE_DEV), jax.random.fold_in(arg_keys[5], 1), 0, NODE_DEV - 1).astype(jnp.int32)
    hub_rows = with_ends(jax.random.randint(arg_keys[6], (HUBS,), 0, NODE_DEV), jax.random.fold_in(arg_keys[6], 1), 0, NODE_DEV - 1).astype(jnp.int32)
    return dict(feat=feat, cotangent=cotangent, weight=weight, nbr_index=nbr_index, degree=degree, send_rows=send_rows, hub_rows=hub_rows)


def silu_slope(pre_act):
    sigmoid_value = jax.nn.sigmoid(pre_act)
    return sigmoid_value * (1.0 + pre_act * (1.0 - sigmoid_value))


def reference(feat, cotangent, weight, nbr_index, degree, send_rows, hub_rows):
    devices = N_REGION * N_SUB
    node_total = NODE_DEV * devices
    feat_width = feat.shape[1]
    hub_global = ((jnp.arange(HUBS, dtype=jnp.int32) // HUB_DEV) * NODE_DEV + hub_rows).astype(jnp.int32)
    send_table = send_rows.reshape(devices, devices, BOUND)
    sources = jnp.arange(devices, dtype=jnp.int32)

    def one_device(device):
        local_ids = device * NODE_DEV + jnp.arange(NODE_DEV, dtype=jnp.int32)
        sent_rows = lax.dynamic_index_in_dim(send_table, device, 1, keepdims=False)
        recv_ids = (sources[:, None] * NODE_DEV + sent_rows).reshape(-1)
        lookup = jnp.concatenate([local_ids, recv_ids, hub_global]).astype(jnp.int32)
        start_row = (device * NODE_DEV).astype(jnp.int32)
        own_nbr = lax.dynamic_slice_in_dim(nbr_index, start_row, NODE_DEV, 0)
        own_deg = lax.dynamic_slice_in_dim(degree, start_row, NODE_DEV, 0)
        own_feat = lax.dynamic_slice_in_dim(feat, start_row, NODE_DEV, 0)
        own_cot = lax.dynamic_slice_in_dim(cotangent, start_row, NODE_DEV, 0)
        global_ids = lookup[own_nbr]
        slot_live = jnp.arange(NBRS, dtype=jnp.int32)[None, :] < own_deg[:, None]
        gathered = feat[global_ids].astype(jnp.float32)
        summed = own_feat.astype(jnp.float32) + jnp.sum(jnp.where(slot_live[:, :, None], gathered, 0.0), axis=1)
        divisor = (own_deg + 1).astype(jnp.float32)[:, None]
        mean_rows = (summed / divisor).astype(jnp.bfloat16)
        pre_act = jnp.dot(mean_rows, weight, preferred_element_type=jnp.float32)
        output_rows = jax.nn.silu(pre_act).astype(jnp.bfloat16)
        act_grad = (own_cot.astype(jnp.float32) * silu_slope(pre_act)).astype(jnp.bfloat16)
        back_proj = jnp.dot(act_grad, weight.T, preferred_element_type=jnp.float32)
        per_target = back_proj / divisor
        dropped = jnp.where(slot_live, global_ids, node_total).astype(jnp.int32)
        return output_rows, per_target, dropped

    outputs, target_terms, targets = lax.map(one_device, sources)
    gradient = target_terms.reshape(node_total, feat_width)

    def accumulate(device, running):
        block_terms = target_terms[device]
        spread = jnp.broadcast_to(block_terms[:, None, :], (NODE_DEV, NBRS, feat_width)).reshape(-1, feat_width)
        return running.at[targets[device].reshape(-1)].add(spread, mode="drop")

    gradient = lax.fori_loop(0, devices, accumulate, gradient)
    return outputs.reshape(node_total, feat_width), gradient.astype(jnp.bfloat16)
```

```python
import jax
import jax.numpy as jnp
from jax import lax
from jax.experimental import pallas as pl
from jax.experimental.pallas import tpu as pltpu
from jax.sharding import PartitionSpec as P

MESH = pl.DeviceIdType.MESH
Y, X, Z = 8, 4, 8
CHIPS = Y * X * Z


def place():
    region = lax.axis_index("region")
    sub = lax.axis_index("sub")
    return region // 2, region % 2, sub // 8, sub % 8


def swap_kernel(send, recv, send_sem, recv_sem):
    y, core, x, z = place()
    chip = y * 32 + x * 8 + z

    def post(step, carry):
        mixed = (step * 77) % 256
        ty, tx, tz = (y + mixed // 32) % 8, (x + (mixed // 8) % 4) % 4, (z + mixed % 8) % 8
        pltpu.make_async_remote_copy(
            src_ref=send.at[ty * 32 + tx * 8 + tz],
            dst_ref=recv.at[chip],
            send_sem=send_sem,
            recv_sem=recv_sem,
            device_id=(ty * 2 + core, tx * 8 + tz),
            device_id_type=MESH,
        ).start()
        return carry

    lax.fori_loop(1, CHIPS, post, 0)
    most = pl.ds(0, CHIPS - 1)
    pltpu.make_async_copy(recv.at[most], recv.at[most], recv_sem).wait()
    pltpu.make_async_copy(send.at[most], send.at[most], send_sem).wait()
    recv[chip] = send[chip]


def swap(tiles):
    return pl.pallas_call(
        swap_kernel,
        out_shape=jax.ShapeDtypeStruct(tiles.shape, tiles.dtype),
        in_specs=[pl.BlockSpec(memory_space=pltpu.VMEM)],
        out_specs=pl.BlockSpec(memory_space=pltpu.VMEM),
        scratch_shapes=[pltpu.SemaphoreType.DMA, pltpu.SemaphoreType.DMA],
        compiler_params=pltpu.CompilerParams(has_side_effects=True, vmem_limit_bytes=32 << 20),
        name="swap",
    )(tiles)


def exchange(rows):
    core = lax.axis_index("region") % 2
    width = rows.shape[-1]
    tiles = rows.reshape(2, Y, 2, X * Z, width).transpose(1, 3, 2, 0, 4).reshape(CHIPS, 32, 128)
    came = swap(tiles).reshape(CHIPS, 2, 2, width)
    mine = lax.dynamic_index_in_dim(came, core, 1, keepdims=False)
    other = lax.dynamic_index_in_dim(came, 1 - core, 1, keepdims=False)
    pairs = [(r, r ^ 1) for r in range(16)]
    other = lax.ppermute(other, "region", pairs)
    first = jnp.where(core == 0, mine, other)
    second = jnp.where(core == 0, other, mine)
    both = jnp.stack([first, second], axis=1)
    return both.reshape(Y, X * Z, 2, 2, width).transpose(3, 0, 2, 1, 4).reshape(2, 512, width)


def silu_slope(pre_act):
    sigmoid_value = jax.nn.sigmoid(pre_act)
    return sigmoid_value * (1.0 + pre_act * (1.0 - sigmoid_value))


def on_device(feat, cotangent, weight, nbr_index, degree, send_rows, hub_rows):
    node_count, feat_width = feat.shape
    full_weight = lax.all_gather(weight, "sub", axis=0, tiled=True)
    own = jnp.arange(node_count, dtype=jnp.int32)
    picks = (send_rows == own[None, :]).astype(jnp.bfloat16)
    bound_out = jnp.dot(picks, feat, preferred_element_type=jnp.float32).astype(jnp.bfloat16)
    hub_out = jnp.broadcast_to(feat[hub_rows], bound_out.shape)
    incoming = exchange(jnp.stack([bound_out, hub_out]))
    lookup = jnp.concatenate([feat, incoming[0], incoming[1]], axis=0)
    columns = jnp.arange(lookup.shape[0], dtype=jnp.int32)
    slots = jnp.arange(nbr_index.shape[1], dtype=jnp.int32)
    live = jnp.where(slots[None, :] < degree[:, None], nbr_index, -1)
    counts = jnp.sum((live[:, :, None] == columns[None, None, :]).astype(jnp.float32), axis=1)
    edges = counts.astype(jnp.bfloat16)
    summed = feat.astype(jnp.float32) + jnp.dot(edges, lookup, preferred_element_type=jnp.float32)
    divisor = (degree + 1).astype(jnp.float32)[:, None]
    mean_rows = (summed / divisor).astype(jnp.bfloat16)
    pre_act = jnp.dot(mean_rows, full_weight, preferred_element_type=jnp.float32)
    output_rows = jax.nn.silu(pre_act).astype(jnp.bfloat16)
    act_grad = (cotangent.astype(jnp.float32) * silu_slope(pre_act)).astype(jnp.bfloat16)
    back_proj = lax.dot_general(
        act_grad, full_weight, (((1,), (1,)), ((), ())), preferred_element_type=jnp.float32
    )
    per_target = back_proj / divisor
    table = lax.dot_general(
        counts, per_target, (((0,), (0,)), ((), ())), precision=lax.Precision.HIGHEST, preferred_element_type=jnp.float32
    )
    own_grad = table[:node_count] + per_target
    outgoing = table[node_count:].astype(jnp.bfloat16).reshape(2, 512, feat_width)
    returned = exchange(outgoing)
    own_grad = own_grad + lax.dot_general(
        picks, returned[0], (((0,), (0,)), ((), ())), preferred_element_type=jnp.float32
    )
    hub_grad = jnp.sum(returned[1].astype(jnp.float32), axis=0)
    own_grad = own_grad + jnp.where((own == hub_rows[0])[:, None], hub_grad[None, :], 0.0)
    return (output_rows, own_grad.astype(jnp.bfloat16))


def solution(mesh):
    placed = (
        P(("region", "sub"), None),
        P(("region", "sub"), None),
        P("sub", None),
        P(("region", "sub"), None),
        P(("region", "sub")),
        P(("region", "sub"), None),
        P(("region", "sub")),
    )
    return jax.shard_map(
        on_device,
        mesh=mesh,
        in_specs=placed,
        out_specs=(P(("region", "sub"), None), P(("region", "sub"), None)),
        check_vma=False,
    )
```

```python
import functools

import jax
import jax.numpy as jnp
from jax import lax
from jax.experimental import pallas as pl
from jax.experimental.pallas import tpu as pltpu
from jax.sharding import PartitionSpec as P

MESH = pl.DeviceIdType.MESH
BF16, F32 = jnp.bfloat16, jnp.float32
Y, X, Z = 8, 4, 8
CHIPS = Y * X * Z
NODES, WIDTH, BOUND, HUBS = 128, 1024, 512, 512
COLUMNS = NODES + BOUND + HUBS
CHUNKS = 4
PAIRS = CHIPS // 2 // CHUNKS


def place():
    region = lax.axis_index("region")
    sub = lax.axis_index("sub")
    return region // 2, region % 2, sub // 8, sub % 8


def device(y, core, x, z):
    return (y * 2 + core, x * 8 + z)


def remote(src, dst, send_sem, recv_sem, target):
    copy = pltpu.make_async_remote_copy(
        src_ref=src, dst_ref=dst, send_sem=send_sem, recv_sem=recv_sem, device_id=target, device_id_type=MESH
    )
    copy.start()


def await_bytes(ref, sem):
    pltpu.make_async_copy(ref, ref, sem).wait()


def dot(a, b):
    return jnp.dot(a, b, preferred_element_type=F32)


def whole_kernel(
    feat, cot, shard, live, divisor, send_row, hub_at,
    out, grad,
    picks_t, wide, full_weight, lookup, edges, edges_t, picks, pre, terms, high, low, own_sum,
    swap_out_f, swap_in_f, post_f, came_f, swap_out_b, swap_in_b, post_b, came_b,
    hub_tile, hub_other, hub_tiles, table, hub_table,
    hub_core, hub_x_out, hub_x_in, hub_x_sum, hub_y_out, hub_y_in, hub_y_sum, hub_z_in, hub_z_sum, hub_last, hub_row,
    swap_recv_f, swap_recv_b, send_sems, recv_sems,
):
    y, core, x, z = place()
    chip = y * 32 + x * 8 + z
    partner = device(y, 1 - core, x, z)
    holds = core == z // 4

    sem_ids = iter(range(32))

    def sems():
        i = next(sem_ids)
        return send_sems.at[i], recv_sems.at[i]

    def target_of(step):
        dz = step % 8
        dy = (step // 8 + step) % 8
        dx = step // 64
        return (y + dy) % 8, (x + dx) % 4, (z + dz) % 8

    def chip_of(at):
        return at[0] * 32 + at[1] * 8 + at[2]

    w_z, w_x, w_core = sems(), sems(), sems()
    half = pl.ds(pl.multiple_of(core * 16, 16), 16)
    for d in range(1, Z):
        remote(shard.at[half], full_weight.at[x, z, core], *w_z, device(y, core, x, (z + d) % 8))
    full_weight[x, z, 0] = shard[0:16]
    full_weight[x, z, 1] = shard[16:32]

    own_id = lax.broadcasted_iota(jnp.int32, (NODES, BOUND), 0)
    one_hot = jnp.where(own_id == send_row[...], 1.0, 0.0)
    picks[...] = one_hot.astype(BF16)
    for b in range(BOUND // 128):
        picks_t[b * 128 : (b + 1) * 128, :] = one_hot[:, b * 128 : (b + 1) * 128].T.astype(BF16)

    def in_tiles(ref, n, part):
        for e in range(2):
            ref[pl.ds(2 * n + e, 512, stride=8), :] = part[:, e * 128 : (e + 1) * 128]

    h_core, h_z, h_y, h_x, h_last = sems(), sems(), sems(), sems(), sems()
    hub_pick = jnp.where(lax.broadcasted_iota(jnp.int32, (16, NODES), 1) == hub_at[0], 1.0, 0.0).astype(BF16)
    hub_wide = dot(hub_pick, feat[...])[0:8]
    lane_group = lax.broadcasted_iota(jnp.int32, (8, 128), 0)
    own_hub = jnp.zeros((8, 128), F32)
    for j in range(8):
        own_hub = jnp.where(lane_group == j, hub_wide[:, j * 128 : (j + 1) * 128], own_hub)
    hub_tile[...] = jnp.concatenate([own_hub, own_hub], axis=0).astype(BF16)
    remote(hub_tile, hub_other, *h_core, partner)

    def swap_start(row, swap_out, swap_in, send_sem, recv_sem):
        for chunk in range(CHUNKS):

            def build(m, carry):
                first = row(chip_of(target_of(2 * m)), 1)
                second = row(chip_of(target_of(2 * m + 1)), 1)
                swap_out[m] = jnp.concatenate([first, second], axis=0).astype(BF16)
                return carry

            lax.fori_loop(chunk * PAIRS, (chunk + 1) * PAIRS, build, 0, unroll=4)
            part = pl.ds(chunk * PAIRS, PAIRS)
            remote(swap_out.at[part], swap_in.at[part], send_sem, recv_sem.at[chunk], partner)

    def post_chunk(chunk, row, swap_in, post, came, swap_recv, send_sem, recv_sem):
        await_bytes(swap_in.at[pl.ds(chunk * PAIRS, PAIRS)], swap_recv.at[chunk])

        def step(m, carry):
            other = swap_in[m].astype(F32)
            for e in range(2):
                i = 2 * m + e
                at = target_of(i)
                tile = jnp.concatenate([row(chip_of(at), 0), other[8 * e : 8 * e + 8]], axis=0).astype(BF16)
                post[i] = tile

                def go():
                    remote(post.at[i], came.at[chip], send_sem, recv_sem, device(at[0], core, at[1], at[2]))

                if e:
                    go()
                else:
                    pl.when(i > 0)(go)
            return carry

        lax.fori_loop(chunk * PAIRS, (chunk + 1) * PAIRS, step, 0)

    def exchange_end(post, came, swap_out, swap_send, send_sem, recv_sem):
        most = pl.ds(0, CHIPS - 1)
        await_bytes(came.at[most], recv_sem)
        came[chip] = post[0]

    def finish_sends(post, swap_out, swap_send, send_sem):
        await_bytes(post.at[pl.ds(0, CHIPS - 1)], send_sem)
        await_bytes(swap_out, swap_send)

    def to_rows(tiles, base):
        for part in range(8):
            wide[part * 512 : (part + 1) * 512, :] = tiles[part * 32 : (part + 1) * 32].reshape(512, 128).astype(F32)
        for j in range(8):
            lookup[base : base + 512, j * 128 : (j + 1) * 128] = wide[pl.ds(j, 512, stride=8), :].astype(BF16)

    bound_f, bound_b, swap_f, swap_b = sems(), sems(), sems(), sems()

    for n in range(4):
        in_tiles(table, n, dot(picks_t[...], feat[:, n * 256 : (n + 1) * 256]))

    def table_row(to_chip, other):
        return table[pl.ds(pl.multiple_of((to_chip * 2 + other) * 8, 8), 8), :]

    swap_start(table_row, swap_out_f, swap_in_f, swap_f[0], swap_recv_f)

    await_bytes(hub_other, h_core[1])
    theirs = hub_other[...].astype(F32)[0:8]
    first = jnp.where(core == 0, own_hub, theirs)
    second = jnp.where(core == 0, theirs, own_hub)
    z_slab = ((x * 2 + core) * 8 + y) * 4

    @pl.when(holds)
    def _():
        slot = z_slab + z % 4
        hub_tiles[slot] = jnp.concatenate([first, second], axis=0).astype(BF16)
        for d in range(1, Z):
            remote(hub_tiles.at[slot], hub_tiles.at[slot], *h_z, device(y, core, x, (z + d) % 8))

    forward = functools.partial(
        post_chunk, row=table_row, swap_in=swap_in_f, post=post_f, came=came_f, swap_recv=swap_recv_f,
        send_sem=bound_f[0], recv_sem=bound_f[1],
    )
    forward(0)

    await_bytes(full_weight.at[0, pl.ds(0, 7), 0], w_z[1])
    for d in range(1, X):
        to = (x + d) % 4
        remote(full_weight.at[x, :, core], full_weight.at[x, :, core], *w_x, device(y, core, to, z))

    @pl.when(holds)
    def _():
        await_bytes(hub_tiles.at[pl.ds(0, 3)], h_z[1])
        await_bytes(hub_tiles.at[pl.ds(0, 7)], h_z[0])

    @pl.when(jnp.logical_not(holds))
    def _():
        await_bytes(hub_tiles.at[pl.ds(0, 4)], h_z[1])

    y_slab = pl.ds(z_slab, 4)
    for d in range(1, Y):
        remote(hub_tiles.at[y_slab], hub_tiles.at[y_slab], *h_y, device((y + d) % 8, core, x, z))
    forward(1)

    await_bytes(hub_tiles.at[pl.ds(0, 28)], h_y[1])
    x_slab = pl.ds((x * 2 + core) * 32, 32)
    for d in range(1, X):
        remote(hub_tiles.at[x_slab], hub_tiles.at[x_slab], *h_x, device(y, core, (x + d) % 4, z))
    forward(2)
    forward(3)

    await_bytes(full_weight.at[pl.ds(0, 3), :, 0], w_x[1])
    remote(full_weight.at[:, :, core], full_weight.at[:, :, core], *w_core, partner)
    await_bytes(hub_tiles.at[pl.ds(0, 96)], h_x[1])
    for at in range(X):
        slab = pl.ds((at * 2 + core) * 32, 32)
        remote(hub_tiles.at[slab], hub_tiles.at[slab], *h_last, partner)

    for b in range(COLUMNS // 128):
        row_id = lax.broadcasted_iota(jnp.int32, (128, 128), 0) + b * 128
        count = jnp.zeros((128, 128), F32)
        for k in range(live.shape[0]):
            count = count + jnp.where(live[k : k + 1, :] == row_id, 1.0, 0.0)
        edges_t[b * 128 : (b + 1) * 128, :] = count.astype(BF16)
        edges[:, b * 128 : (b + 1) * 128] = count.T.astype(BF16)
    lookup[0:NODES, :] = feat[...]
    await_bytes(hub_tiles.at[pl.ds(0, 128)], h_last[1])
    to_rows(hub_tiles, NODES + BOUND)
    await_bytes(full_weight.at[:, :, 0], w_core[1])
    exchange_end(post_f, came_f, swap_out_f, swap_f[0], *bound_f)
    to_rows(came_f, NODES)

    div = divisor[...]
    for n in range(4):
        cols = slice(n * 256, (n + 1) * 256)
        summed = feat[:, cols].astype(F32) + dot(edges[...], lookup[:, cols])
        high[:, cols] = (summed / div).astype(BF16)
    for n in range(4):
        cols = slice(n * 256, (n + 1) * 256)
        total = jnp.zeros((NODES, 256), F32)
        for k in range(X):
            total = total + dot(high[:, k * 256 : (k + 1) * 256], full_weight[k, :, :, :, cols].reshape(256, 256))
        sig = jax.nn.sigmoid(total)
        out[:, cols] = (total * sig).astype(BF16)
        slope = sig * (1.0 + total * (1.0 - sig))
        pre[:, cols] = (cot[:, cols].astype(F32) * slope).astype(BF16)
    for n in range(X):
        cols = slice(n * 256, (n + 1) * 256)
        term = lax.dot_general(
            pre[...], full_weight[n].reshape(256, WIDTH), (((1,), (1,)), ((), ())), preferred_element_type=F32
        ) / div
        top = term.astype(BF16)
        terms[:, cols] = term
        high[:, cols] = top
        low[:, cols] = (term - top.astype(F32)).astype(BF16)

    def spread(rows, ref):
        for n in range(4):
            cols = slice(n * 256, (n + 1) * 256)
            in_tiles(ref, n, dot(edges_t[rows, :], high[:, cols]) + dot(edges_t[rows, :], low[:, cols]))

    g_core, g_x, g_y, g_z, g_last = sems(), sems(), sems(), sems(), sems()
    spread(slice(NODES + BOUND, COLUMNS), hub_table)
    for at in range(X):
        slab = pl.ds(pl.multiple_of((at * 2 + 1 - core) * 512, 512), 512)
        remote(hub_table.at[slab], hub_core.at[at], *g_core, partner)

    spread(slice(NODES, NODES + BOUND), table)

    swap_start(table_row, swap_out_b, swap_in_b, swap_b[0], swap_recv_b)
    backward = functools.partial(
        post_chunk, row=table_row, swap_in=swap_in_b, post=post_b, came=came_b, swap_recv=swap_recv_b,
        send_sem=bound_b[0], recv_sem=bound_b[1],
    )

    def kept(at):
        return hub_table[pl.ds(pl.multiple_of((at * 2 + core) * 512, 512), 512), :] + hub_core[at]

    await_bytes(hub_core, g_core[1])
    for d in range(1, X):
        to = (x + d) % 4
        hub_x_out[d - 1] = kept(to).astype(BF16)
        remote(hub_x_out.at[d - 1], hub_x_in.at[d - 1], *g_x, device(y, core, to, z))
    backward(0)
    backward(1)

    await_bytes(hub_x_in, g_x[1])
    part = kept(x)
    for d in range(X - 1):
        part = part + hub_x_in[d].astype(F32)
    hub_x_sum[...] = part
    hub_y_out[...] = part.astype(BF16).reshape(Y, 64, 128)
    for d in range(1, Y):
        to = (y + d) % 8
        remote(hub_y_out.at[to], hub_y_in.at[d - 1], *g_y, device(to, core, x, z))
    backward(2)

    await_bytes(hub_y_in, g_y[1])
    part = hub_x_sum[pl.ds(pl.multiple_of(y * 64, 64), 64), :]
    for d in range(Y - 1):
        part = part + hub_y_in[d].astype(F32)
    hub_y_sum[...] = part
    for at in range(4):
        to = core * 4 + at

        @pl.when(to != z)
        def _():
            slot = (to - z + 8) % 8 - 1
            remote(hub_y_sum.at[pl.ds(at * 16, 16)], hub_z_in.at[slot], *g_z, device(y, core, x, to))

    backward(3)

    @pl.when(holds)
    def _():
        await_bytes(hub_z_in, g_z[1])
        total = hub_y_sum[pl.ds(pl.multiple_of((z % 4) * 16, 16), 16), :]
        for d in range(Z - 1):
            total = total + hub_z_in[d]
        hub_z_sum[...] = total
        remote(hub_z_sum, hub_last, *g_last, partner)
        hub_row[...] = hub_z_sum[pl.ds(pl.multiple_of(core * 8, 8), 8), :]
        await_bytes(hub_z_in.at[pl.ds(0, 3)], g_z[0])
        await_bytes(hub_z_sum, g_last[0])

    @pl.when(jnp.logical_not(holds))
    def _():
        await_bytes(hub_last, g_last[1])
        hub_row[...] = hub_last[pl.ds(pl.multiple_of(core * 8, 8), 8), :]
        await_bytes(hub_z_in.at[pl.ds(0, 4)], g_z[0])

    hub_mask = lax.broadcasted_iota(jnp.int32, (NODES, 128), 0) == hub_at[0]
    for n in range(4):
        cols = slice(n * 256, (n + 1) * 256)
        own_sum[:, cols] = (
            terms[:, cols] + dot(edges_t[0:NODES, :], high[:, cols]) + dot(edges_t[0:NODES, :], low[:, cols])
        )
    for j in range(8):
        cols = slice(j * 128, (j + 1) * 128)
        own_sum[:, cols] += jnp.where(hub_mask, hub_row[j : j + 1, :], 0.0)
    exchange_end(post_b, came_b, swap_out_b, swap_b[0], *bound_b)
    to_rows(came_b, NODES)
    for n in range(4):
        cols = slice(n * 256, (n + 1) * 256)
        grad[:, cols] = (own_sum[:, cols] + dot(picks[...], lookup[NODES : NODES + BOUND, cols])).astype(BF16)

    for d in range(1, Z):
        await_bytes(shard.at[half], w_z[0])
    await_bytes(full_weight.at[pl.ds(0, 3), :, 0], w_x[0])
    await_bytes(full_weight.at[:, :, 0], w_core[0])
    await_bytes(hub_tile, h_core[0])
    await_bytes(hub_tiles.at[pl.ds(0, 28)], h_y[0])
    await_bytes(hub_tiles.at[pl.ds(0, 96)], h_x[0])
    await_bytes(hub_tiles.at[pl.ds(0, 128)], h_last[0])
    await_bytes(hub_core, g_core[0])
    await_bytes(hub_x_in, g_x[0])
    await_bytes(hub_y_in, g_y[0])
    finish_sends(post_f, swap_out_f, swap_f[0], bound_f[0])
    finish_sends(post_b, swap_out_b, swap_b[0], bound_b[0])


def tiles(count):
    return pltpu.VMEM((count, 16, 128), BF16)


SCRATCH = [
    pltpu.VMEM((BOUND, NODES), BF16),
    pltpu.VMEM((4096, 128), F32),
    pltpu.VMEM((X, Z, 2, 16, WIDTH), BF16),
    pltpu.VMEM((COLUMNS, WIDTH), BF16),
    pltpu.VMEM((NODES, COLUMNS), BF16),
    pltpu.VMEM((COLUMNS, NODES), BF16),
    pltpu.VMEM((NODES, BOUND), BF16),
    pltpu.VMEM((NODES, WIDTH), BF16),
    pltpu.VMEM((NODES, WIDTH), F32),
    pltpu.VMEM((NODES, WIDTH), BF16),
    pltpu.VMEM((NODES, WIDTH), BF16),
    pltpu.VMEM((NODES, WIDTH), F32),
    tiles(128), tiles(128), tiles(256), tiles(256),
    tiles(128), tiles(128), tiles(256), tiles(256),
    pltpu.VMEM((16, 128), BF16),
    pltpu.VMEM((16, 128), BF16),
    tiles(256),
    pltpu.VMEM((4096, 128), F32),
    pltpu.VMEM((4096, 128), F32),
    pltpu.VMEM((X, 512, 128), F32),
    pltpu.VMEM((X - 1, 512, 128), BF16),
    pltpu.VMEM((X - 1, 512, 128), BF16),
    pltpu.VMEM((512, 128), F32),
    pltpu.VMEM((Y, 64, 128), BF16),
    pltpu.VMEM((Y - 1, 64, 128), BF16),
    pltpu.VMEM((64, 128), F32),
    pltpu.VMEM((Z - 1, 16, 128), F32),
    pltpu.VMEM((16, 128), F32),
    pltpu.VMEM((16, 128), F32),
    pltpu.VMEM((8, 128), F32),
    pltpu.SemaphoreType.DMA((CHUNKS,)),
    pltpu.SemaphoreType.DMA((CHUNKS,)),
    pltpu.SemaphoreType.DMA((20,)),
    pltpu.SemaphoreType.DMA((20,)),
]


def on_device(feat, cotangent, weight, nbr_index, degree, send_rows, hub_rows):
    core = lax.axis_index("region") % 2
    s = nbr_index - NODES
    bound_column = NODES + ((s // 64) * 32 + s % 32) * 2 + ((s // 32) % 2 + core) % 2
    h = nbr_index - (NODES + BOUND)
    hub_column = (
        NODES + BOUND
        + ((((h % 32) // 8 * 2 + (h % 8) // 4) * 8 + h // 64) * 4 + h % 4) * 2
        + (h // 32) % 2
    )
    column = jnp.where(
        nbr_index < NODES, nbr_index, jnp.where(nbr_index < NODES + BOUND, bound_column, hub_column)
    )
    slots = jnp.arange(nbr_index.shape[1], dtype=jnp.int32)
    live = jnp.where(slots[None, :] < degree[:, None], column, -1).T
    divisor = (degree + 1).astype(F32)[:, None]
    by_core = send_rows.reshape(Y, 2, 32)
    by_core = jnp.where(core == 0, by_core, by_core[:, ::-1])
    send_at = by_core.transpose(0, 2, 1).reshape(BOUND)
    vmem = pl.BlockSpec(memory_space=pltpu.VMEM)
    smem = pl.BlockSpec(memory_space=pltpu.SMEM)
    return pl.pallas_call(
        whole_kernel,
        out_shape=(
            jax.ShapeDtypeStruct((NODES, WIDTH), BF16),
            jax.ShapeDtypeStruct((NODES, WIDTH), BF16),
        ),
        in_specs=[vmem] * 6 + [smem],
        out_specs=(vmem, vmem),
        scratch_shapes=SCRATCH,
        compiler_params=pltpu.CompilerParams(has_side_effects=True, vmem_limit_bytes=48 << 20),
        name="sage",
    )(feat, cotangent, weight, live, divisor, send_at[None, :], hub_rows)


def solution(mesh):
    placed = (
        P(("region", "sub"), None),
        P(("region", "sub"), None),
        P("sub", None),
        P(("region", "sub"), None),
        P(("region", "sub")),
        P(("region", "sub"), None),
        P(("region", "sub")),
    )
    return jax.shard_map(
        on_device,
        mesh=mesh,
        in_specs=placed,
        out_specs=(P(("region", "sub"), None), P(("region", "sub"), None)),
        check_vma=False,
    )
```

```python
import jax
import jax.numpy as jnp
from jax import lax
from jax.experimental import pallas as pl
from jax.experimental.pallas import tpu as pltpu
from jax.sharding import PartitionSpec as P

MESH = pl.DeviceIdType.MESH
BF16, F32, I32 = jnp.bfloat16, jnp.float32, jnp.int32
Y, X, Z = 8, 4, 8
CHIPS = Y * X * Z
PLANE = Y * Z
NODES, WIDTH, BOUND, HUBS = 128, 1024, 512, 512
COLUMNS = NODES + BOUND + HUBS
STEPS = (2, 1, 3, 0)


def place():
    region = lax.axis_index("region")
    sub = lax.axis_index("sub")
    return region // 2, region % 2, sub // 8, sub % 8


def device(y, core, x, z):
    return (y * 2 + core, x * 8 + z)


def remote(src, dst, sems, target):
    pltpu.make_async_remote_copy(
        src_ref=src, dst_ref=dst, send_sem=sems[0], recv_sem=sems[1], device_id=target, device_id_type=MESH
    ).start()


def await_bytes(ref, sem):
    pltpu.make_async_copy(ref, ref, sem).wait()


def dot(a, b):
    return jnp.dot(a, b, preferred_element_type=F32)


def block(n):
    return slice(n * 256, (n + 1) * 256)


def whole_kernel(
    feat, cot, shard, nbr_t, degree, send_row, hub_at,
    out, grad,
    pick_rows, picks, table, wide, full_weight, edges, edges_t, hub_lookup, div, total, mean, act, terms, high, low, own_sum,
    swap_out_f, swap_in_f, post_f, came_f, swap_out_b, swap_in_b, post_b, came_b,
    hub_tile, hub_other, hub_tiles, hub_table,
    hub_core, hub_x_out, hub_x_in, hub_x_sum, hub_y_out, hub_y_in, hub_y_sum, hub_z_in, hub_z_sum, hub_last, hub_row,
    send_sems, recv_sems, entered,
):
    y, core, x, z = place()
    chip = x * PLANE + y * 8 + z
    partner = device(y, 1 - core, x, z)
    holds = core == z // 4
    sem_ids = iter(range(64))
    due = {}
    sent = []

    def sems():
        i = next(sem_ids)
        return send_sems.at[i], recv_sems.at[i]

    def expect(name, ref, sem):
        due[name] = lambda: await_bytes(ref, sem)

    def settle(name):
        due.pop(name)()

    def leaves(ref, sem):
        sent.append(lambda: await_bytes(ref, sem))

    barrier = pltpu.get_barrier_semaphore()
    y_line = [device((y + d) % 8, core, x, z) for d in range(1, Y)]
    z_line = [device(y, core, x, (z + d) % 8) for d in range(1, Z)]
    x_line = [device(y, core, (x + d) % 4, z) for d in range(1, X)]
    for other in [partner] + x_line + y_line + z_line:
        pl.semaphore_signal(barrier, inc=1, device_id=other, device_id_type=MESH)

    own_id = lax.broadcasted_iota(I32, (NODES, 128), 0)
    for b in range(BOUND // 128):
        one_hot = jnp.where(own_id == send_row[:, b * 128 : (b + 1) * 128], 1.0, 0.0)
        pick_rows[b * 128 : (b + 1) * 128, :] = one_hot.T
    hub_pick = jnp.where(lax.broadcasted_iota(I32, (16, NODES), 1) == hub_at[0], 1.0, 0.0).astype(BF16)
    hub_wide = dot(hub_pick, feat[...])[0:8]
    lane_group = lax.broadcasted_iota(I32, (8, 128), 0)
    own_hub = jnp.zeros((8, 128), F32)
    for j in range(8):
        own_hub = jnp.where(lane_group == j, hub_wide[:, j * 128 : (j + 1) * 128], own_hub)
    hub_tile[...] = jnp.concatenate([own_hub, own_hub], axis=0).astype(BF16)
    pl.semaphore_wait(barrier, len(x_line) + len(y_line) + len(z_line) + 1)

    w_z, w_x, w_core = sems(), sems(), sems()
    half = pl.ds(pl.multiple_of(core * 16, 16), 16)
    for other in z_line:
        remote(shard.at[half], full_weight.at[x, z, core], w_z, other)
    expect("w_z", full_weight.at[0, pl.ds(0, 7), 0], w_z[1])
    leaves(full_weight.at[0, pl.ds(0, 7), 0], w_z[0])
    for other in y_line:
        pl.semaphore_signal(entered.at[0], inc=1, device_id=other, device_id_type=MESH)
    h_core, h_z, h_y, h_x, h_last = sems(), sems(), sems(), sems(), sems()
    remote(hub_tile, hub_other, h_core, partner)
    expect("h_core", hub_other, h_core[1])
    leaves(hub_tile, h_core[0])
    full_weight[x, z, 0] = shard[0:16]
    full_weight[x, z, 1] = shard[16:32]

    def in_tiles(ref, base, n, part):
        for e in range(2):
            ref[pl.ds(base + 2 * n + e, part.shape[0], stride=8), :] = part[:, e * 128 : (e + 1) * 128]

    def table_row(to, which):
        row = to[1] * 128 + which * 64 + to[0] * 8 + to[2]
        return table[pl.ds(pl.multiple_of(row * 8, 8), 8), :]

    def target_of(k, i):
        return (y + i // 8 + i) % 8, (x + STEPS[k]) % 4, (z + i) % 8

    def swap_start(k, swap_out, swap_in, pair):
        def build(m, carry):
            first = table_row(target_of(k, 2 * m), 1)
            second = table_row(target_of(k, 2 * m + 1), 1)
            swap_out[k * 32 + m] = jnp.concatenate([first, second], axis=0).astype(BF16)
            return carry

        lax.fori_loop(0, 32, build, 0, unroll=4)
        part = pl.ds(k * 32, 32)
        remote(swap_out.at[part], swap_in.at[part], pair, partner)
        expect(("swap", k), swap_in.at[part], pair[1])
        leaves(swap_out.at[part], pair[0])

    def post_quarter(k, swap_in, post, came, pair):
        settle(("swap", k))

        def step(m, carry):
            theirs = swap_in[k * 32 + m].astype(F32)
            for e in range(2):
                i = 2 * m + e
                to = target_of(k, i)
                tile = jnp.concatenate([table_row(to, 0), theirs[8 * e : 8 * e + 8]], axis=0).astype(BF16)
                at = k * 64 + i

                def go():
                    post[at] = tile
                    remote(post.at[at], came.at[chip], pair, device(to[0], core, to[1], to[2]))

                if e or STEPS[k]:
                    go()
                else:
                    pl.when(i > 0)(go)

                    @pl.when(i == 0)
                    def _():
                        came[chip] = tile
            return carry

        lax.fori_loop(0, 32, step, 0)
        count = 64 if STEPS[k] else 63
        expect(("came", k), came.at[pl.ds(0, count)], pair[1])
        leaves(post.at[pl.ds(0, count)], pair[0])

    def received(k, came):
        settle(("came", k))
        from_x = (x + 4 - STEPS[k]) % 4
        for part in range(4):
            wide[part * 256 : (part + 1) * 256, :] = (
                came[pl.ds(from_x * 64 + part * 16, 16)].reshape(256, 128).astype(F32)
            )

        def columns(n):
            sides = []
            for j in (2 * n, 2 * n + 1):
                sides.append(
                    jnp.concatenate([wide[pl.ds(w * 8 + j, 64, stride=16), :] for w in range(2)], axis=0)
                )
            return jnp.concatenate(sides, axis=1).astype(BF16)

        return from_x, columns

    swaps_f = [sems() for _ in STEPS]
    bounds_f = [sems() for _ in STEPS]

    def select(k):
        to_x = (x + STEPS[k]) % 4
        rows = []
        for which in range(2):
            other = (core + which) % 2
            for to_y in range(Y):
                rows.append(pick_rows[pl.ds(pl.multiple_of(to_y * 64 + other * 32 + to_x * 8, 8), 8), :])
        chosen = jnp.concatenate(rows, axis=0)
        picks[to_x] = chosen.T.astype(BF16)
        chosen = chosen.astype(BF16)
        for n in range(4):
            in_tiles(table, to_x * 1024, n, dot(chosen, feat[:, block(n)]))
        swap_start(k, swap_out_f, swap_in_f, swaps_f[k])

    select(0)

    settle("h_core")
    theirs = hub_other[...].astype(F32)[0:8]
    first = jnp.where(core == 0, own_hub, theirs)
    second = jnp.where(core == 0, theirs, own_hub)
    z_slab = ((x * 2 + core) * 8 + y) * 4

    @pl.when(holds)
    def _():
        slot = z_slab + z % 4
        hub_tiles[slot] = jnp.concatenate([first, second], axis=0).astype(BF16)
        for other in z_line:
            remote(hub_tiles.at[slot], hub_tiles.at[slot], h_z, other)

    def hub_z_due():
        @pl.when(holds)
        def _():
            await_bytes(hub_tiles.at[pl.ds(0, 3)], h_z[1])

        @pl.when(jnp.logical_not(holds))
        def _():
            await_bytes(hub_tiles.at[pl.ds(0, 4)], h_z[1])

    def hub_z_left():
        @pl.when(holds)
        def _():
            await_bytes(hub_tiles.at[pl.ds(0, 7)], h_z[0])

    due["h_z"] = hub_z_due
    sent.append(hub_z_left)
    pl.semaphore_wait(entered.at[0], Y - 1)
    for other in z_line:
        pl.semaphore_signal(entered.at[1], inc=1, device_id=other, device_id_type=MESH)
    select(1)
    pl.semaphore_wait(entered.at[1], Z - 1)
    post_quarter(0, swap_in_f, post_f, came_f, bounds_f[0])
    select(2)

    settle("w_z")
    for other in x_line:
        remote(full_weight.at[x, :, core], full_weight.at[x, :, core], w_x, other)
    expect("w_x", full_weight.at[pl.ds(0, 3), :, 0], w_x[1])
    leaves(full_weight.at[pl.ds(0, 3), :, 0], w_x[0])
    settle("h_z")
    y_slab = pl.ds(z_slab, 4)
    for other in y_line:
        remote(hub_tiles.at[y_slab], hub_tiles.at[y_slab], h_y, other)
    expect("h_y", hub_tiles.at[pl.ds(0, 28)], h_y[1])
    leaves(hub_tiles.at[pl.ds(0, 28)], h_y[0])
    post_quarter(1, swap_in_f, post_f, came_f, bounds_f[1])
    select(3)

    settle("h_y")
    x_slab = pl.ds((x * 2 + core) * 32, 32)
    for other in x_line:
        remote(hub_tiles.at[x_slab], hub_tiles.at[x_slab], h_x, other)
    expect("h_x", hub_tiles.at[pl.ds(0, 96)], h_x[1])
    leaves(hub_tiles.at[pl.ds(0, 96)], h_x[0])
    post_quarter(2, swap_in_f, post_f, came_f, bounds_f[2])
    post_quarter(3, swap_in_f, post_f, came_f, bounds_f[3])

    settle("h_x")
    for at in range(X):
        slab = pl.ds((at * 2 + core) * 32, 32)
        remote(hub_tiles.at[slab], hub_tiles.at[slab], h_last, partner)
    expect("h_last", hub_tiles.at[pl.ds(0, 128)], h_last[1])
    leaves(hub_tiles.at[pl.ds(0, 128)], h_last[0])
    settle("w_x")
    remote(full_weight.at[:, :, core], full_weight.at[:, :, core], w_core, partner)
    expect("w_core", full_weight.at[:, :, 0], w_core[1])
    leaves(full_weight.at[:, :, 0], w_core[0])

    number = nbr_t[...]
    s = number - NODES
    bound_column = (
        NODES + ((s >> 3) & 3) * 128 + (((s >> 5) + core) & 1) * 64 + (s >> 6) * 8 + (s & 7)
    )
    h = number - (NODES + BOUND)
    hub_column = (
        NODES + BOUND
        + ((((h >> 3) & 3) * 2 + ((h >> 2) & 1)) * 32 + (h >> 6) * 4 + (h & 3)) * 2
        + ((h >> 5) & 1)
    )
    column = jnp.where(number < NODES, number, jnp.where(number < NODES + BOUND, bound_column, hub_column))
    slot_id = lax.broadcasted_iota(I32, number.shape, 0)
    live = jnp.where(slot_id < degree[...], column, -1)
    for b in range(COLUMNS // 128):
        row_id = own_id + b * 128
        count = jnp.zeros((128, 128), F32)
        for k in range(live.shape[0]):
            count = count + jnp.where(live[k : k + 1, :] == row_id, 1.0, 0.0)
        edges_t[b * 128 : (b + 1) * 128, :] = count.astype(BF16)
        edges[:, b * 128 : (b + 1) * 128] = count.T.astype(BF16)
    div[...] = jnp.broadcast_to((degree[...] + 1).astype(F32), (128, 128)).T
    for n in range(4):
        rows = feat[:, block(n)]
        total[:, block(n)] = rows.astype(F32) + dot(edges[:, 0:NODES], rows)

    settle("h_last")
    for part in range(8):
        hub_table[part * 512 : (part + 1) * 512, :] = (
            hub_tiles[part * 32 : (part + 1) * 32].reshape(512, 128).astype(F32)
        )
    for j in range(8):
        hub_lookup[:, j * 128 : (j + 1) * 128] = hub_table[pl.ds(j, HUBS, stride=8), :].astype(BF16)
    for n in range(4):
        total[:, block(n)] += dot(edges[:, NODES + BOUND : COLUMNS], hub_lookup[:, block(n)])
    settle("w_core")

    for k in range(X):
        from_x, rows = received(k, came_f)
        part = edges[:, pl.ds(pl.multiple_of(NODES + from_x * 128, 128), 128)]
        for n in range(4):
            total[:, block(n)] += dot(part, rows(n))

    two_div = jnp.concatenate([div[...], div[...]], axis=1)
    for n in range(4):
        mean[:, block(n)] = (total[:, block(n)] / two_div).astype(BF16)
    for n in range(4):
        pre_act = jnp.zeros((NODES, 256), F32)
        for k in range(X):
            pre_act = pre_act + dot(mean[:, block(k)], full_weight[k, :, :, :, block(n)].reshape(256, 256))
        sig = jax.nn.sigmoid(pre_act)
        out[:, block(n)] = (pre_act * sig).astype(BF16)
        slope = sig * (1.0 + pre_act * (1.0 - sig))
        act[:, block(n)] = (cot[:, block(n)].astype(F32) * slope).astype(BF16)
    for n in range(X):
        term = lax.dot_general(
            act[...], full_weight[n].reshape(256, WIDTH), (((1,), (1,)), ((), ())), preferred_element_type=F32
        ) / two_div
        top = term.astype(BF16)
        terms[:, block(n)] = term
        high[:, block(n)] = top
        low[:, block(n)] = (term - top.astype(F32)).astype(BF16)

    def spread(rows, ref, base):
        edge = edges_t[rows, :]
        for n in range(4):
            in_tiles(ref, base, n, dot(edge, high[:, block(n)]) + dot(edge, low[:, block(n)]))

    swaps_b = [sems() for _ in STEPS]
    bounds_b = [sems() for _ in STEPS]
    g_core, g_x, g_y, g_z, g_last = sems(), sems(), sems(), sems(), sems()

    def give_back(k):
        to_x = (x + STEPS[k]) % 4
        spread(pl.ds(pl.multiple_of(NODES + to_x * 128, 128), 128), table, to_x * 1024)
        swap_start(k, swap_out_b, swap_in_b, swaps_b[k])

    give_back(0)

    spread(slice(NODES + BOUND, COLUMNS), hub_table, 0)
    for at in range(X):
        slab = pl.ds(pl.multiple_of((at * 2 + 1 - core) * 512, 512), 512)
        remote(hub_table.at[slab], hub_core.at[at], g_core, partner)
    expect("g_core", hub_core, g_core[1])
    leaves(hub_core, g_core[0])
    give_back(1)
    post_quarter(0, swap_in_b, post_b, came_b, bounds_b[0])

    def kept(at):
        return hub_table[pl.ds(pl.multiple_of((at * 2 + core) * 512, 512), 512), :] + hub_core[at]

    settle("g_core")
    for d in range(1, X):
        hub_x_out[d - 1] = kept((x + d) % 4).astype(BF16)
        remote(hub_x_out.at[d - 1], hub_x_in.at[d - 1], g_x, x_line[d - 1])
    expect("g_x", hub_x_in, g_x[1])
    leaves(hub_x_in, g_x[0])
    give_back(2)
    post_quarter(1, swap_in_b, post_b, came_b, bounds_b[1])
    give_back(3)

    settle("g_x")
    part = kept(x)
    for d in range(X - 1):
        part = part + hub_x_in[d].astype(F32)
    hub_x_sum[...] = part
    hub_y_out[...] = part.astype(BF16).reshape(Y, 64, 128)
    for d in range(1, Y):
        remote(hub_y_out.at[(y + d) % 8], hub_y_in.at[d - 1], g_y, y_line[d - 1])
    expect("g_y", hub_y_in, g_y[1])
    leaves(hub_y_in, g_y[0])
    post_quarter(2, swap_in_b, post_b, came_b, bounds_b[2])
    post_quarter(3, swap_in_b, post_b, came_b, bounds_b[3])

    for n in range(4):
        cols = block(n)
        own_sum[:, cols] = terms[:, cols] + dot(edges_t[0:NODES, :], high[:, cols]) + dot(edges_t[0:NODES, :], low[:, cols])
    settle("g_y")
    part = hub_x_sum[pl.ds(pl.multiple_of(y * 64, 64), 64), :]
    for d in range(Y - 1):
        part = part + hub_y_in[d].astype(F32)
    hub_y_sum[...] = part
    for at in range(4):
        to = core * 4 + at

        @pl.when(to != z)
        def _():
            slot = (to - z + 8) % 8 - 1
            remote(hub_y_sum.at[pl.ds(at * 16, 16)], hub_z_in.at[slot], g_z, device(y, core, x, to))

    for k in range(2):
        from_x, rows = received(k, came_b)
        for n in range(4):
            own_sum[:, block(n)] += dot(picks[from_x], rows(n))

    @pl.when(holds)
    def _():
        await_bytes(hub_z_in, g_z[1])
        here = hub_y_sum[pl.ds(pl.multiple_of((z % 4) * 16, 16), 16), :]
        for d in range(Z - 1):
            here = here + hub_z_in[d]
        hub_z_sum[...] = here
        remote(hub_z_sum, hub_last, g_last, partner)
        hub_row[...] = hub_z_sum[pl.ds(pl.multiple_of(core * 8, 8), 8), :]
        await_bytes(hub_z_in.at[pl.ds(0, 3)], g_z[0])
        await_bytes(hub_z_sum, g_last[0])

    @pl.when(jnp.logical_not(holds))
    def _():
        await_bytes(hub_last, g_last[1])
        hub_row[...] = hub_last[pl.ds(pl.multiple_of(core * 8, 8), 8), :]
        await_bytes(hub_z_in.at[pl.ds(0, 4)], g_z[0])

    hub_mask = own_id == hub_at[0]
    for j in range(8):
        cols = slice(j * 128, (j + 1) * 128)
        own_sum[:, cols] += jnp.where(hub_mask, hub_row[j : j + 1, :], 0.0)

    from_x, rows = received(2, came_b)
    for n in range(4):
        own_sum[:, block(n)] += dot(picks[from_x], rows(n))
    from_x, rows = received(3, came_b)
    for n in range(4):
        grad[:, block(n)] = (own_sum[:, block(n)] + dot(picks[from_x], rows(n))).astype(BF16)
    for wait in sent:
        wait()


def tiles(count):
    return pltpu.VMEM((count, 16, 128), BF16)


SCRATCH = [
    pltpu.VMEM((BOUND, NODES), F32),
    pltpu.VMEM((X, NODES, 128), BF16),
    pltpu.VMEM((4096, 128), F32),
    pltpu.VMEM((1024, 128), F32),
    pltpu.VMEM((X, Z, 2, 16, WIDTH), BF16),
    pltpu.VMEM((NODES, COLUMNS), BF16),
    pltpu.VMEM((COLUMNS, NODES), BF16),
    pltpu.VMEM((HUBS, WIDTH), BF16),
    pltpu.VMEM((128, 128), F32),
    pltpu.VMEM((NODES, WIDTH), F32),
    pltpu.VMEM((NODES, WIDTH), BF16),
    pltpu.VMEM((NODES, WIDTH), BF16),
    pltpu.VMEM((NODES, WIDTH), F32),
    pltpu.VMEM((NODES, WIDTH), BF16),
    pltpu.VMEM((NODES, WIDTH), BF16),
    pltpu.VMEM((NODES, WIDTH), F32),
    tiles(128), tiles(128), tiles(256), tiles(256),
    tiles(128), tiles(128), tiles(256), tiles(256),
    pltpu.VMEM((16, 128), BF16),
    pltpu.VMEM((16, 128), BF16),
    tiles(256),
    pltpu.VMEM((4096, 128), F32),
    pltpu.VMEM((X, 512, 128), F32),
    pltpu.VMEM((X - 1, 512, 128), BF16),
    pltpu.VMEM((X - 1, 512, 128), BF16),
    pltpu.VMEM((512, 128), F32),
    pltpu.VMEM((Y, 64, 128), BF16),
    pltpu.VMEM((Y - 1, 64, 128), BF16),
    pltpu.VMEM((64, 128), F32),
    pltpu.VMEM((Z - 1, 16, 128), F32),
    pltpu.VMEM((16, 128), F32),
    pltpu.VMEM((16, 128), F32),
    pltpu.VMEM((8, 128), F32),
    pltpu.SemaphoreType.DMA((32,)),
    pltpu.SemaphoreType.DMA((32,)),
    pltpu.SemaphoreType.REGULAR((2,)),
]


def on_device(feat, cotangent, weight, nbr_index, degree, send_rows, hub_rows):
    vmem = pl.BlockSpec(memory_space=pltpu.VMEM)
    smem = pl.BlockSpec(memory_space=pltpu.SMEM)
    return pl.pallas_call(
        whole_kernel,
        out_shape=(
            jax.ShapeDtypeStruct((NODES, WIDTH), BF16),
            jax.ShapeDtypeStruct((NODES, WIDTH), BF16),
        ),
        in_specs=[vmem] * 6 + [smem],
        out_specs=(vmem, vmem),
        scratch_shapes=SCRATCH,
        compiler_params=pltpu.CompilerParams(has_side_effects=True, collective_id=0, vmem_limit_bytes=48 << 20),
        name="sage",
    )(feat, cotangent, weight, nbr_index.T, degree[None, :], send_rows.T, hub_rows)


def solution(mesh):
    placed = (
        P(("region", "sub"), None),
        P(("region", "sub"), None),
        P("sub", None),
        P(("region", "sub"), None),
        P(("region", "sub")),
        P(("region", "sub"), None),
        P(("region", "sub")),
    )
    return jax.shard_map(
        on_device,
        mesh=mesh,
        in_specs=placed,
        out_specs=(P(("region", "sub"), None), P(("region", "sub"), None)),
        check_vma=False,
    )
```

```python
import jax
import jax.numpy as jnp
from jax import lax
from jax.experimental import pallas as pl
from jax.experimental.pallas import tpu as pltpu
from jax.sharding import PartitionSpec as P

MESH = pl.DeviceIdType.MESH
BF16, F32, I32 = jnp.bfloat16, jnp.float32, jnp.int32
Y, X, Z = 8, 4, 8
CHIPS = Y * X * Z
PLANE = Y * Z
NODES, WIDTH, BOUND, HUBS = 128, 1024, 512, 512
COLUMNS = NODES + BOUND + HUBS
GROUPS = (2, 1, 3, 0)


def place():
    region = lax.axis_index("region")
    sub = lax.axis_index("sub")
    return region // 2, region % 2, sub // 8, sub % 8


def device(y, core, x, z):
    return (y * 2 + core, x * 8 + z)


def remote(src, dst, sems, target):
    pltpu.make_async_remote_copy(
        src_ref=src, dst_ref=dst, send_sem=sems[0], recv_sem=sems[1], device_id=target, device_id_type=MESH
    ).start()


def await_bytes(ref, sem):
    pltpu.make_async_copy(ref, ref, sem).wait()


def dot(a, b):
    return jnp.dot(a, b, preferred_element_type=F32)


def block(n):
    return slice(n * 256, (n + 1) * 256)


def whole_kernel(
    feat_hbm, cot_hbm, shard_hbm, nbr_hbm, degree_hbm, send_hbm, hub_at,
    out, grad,
    feat, cot, shard, nbr_t, degree, send_row,
    pick_rows, picks, table, wide, full_weight, edges, edges_t, hub_lookup, div, total, mean, act, terms, high, low, own_sum,
    swap_out_f, swap_in_f, stage_f, mid_f, came_f, swap_out_b, swap_in_b, stage_b, mid_b, came_b,
    hub_tile, hub_other, hub_tiles, hub_table,
    hub_core, hub_x_out, hub_x_in, hub_x_sum, hub_y_out, hub_y_in, hub_y_sum, hub_z_in, hub_z_sum, hub_last, hub_row,
    send_sems, recv_sems, load_sems, entered,
):
    y, core, x, z = place()
    slot_y = (y % 4) * 2 + y // 4
    partner = device(y, 1 - core, x, z)
    holds = core == z // 4
    sem_ids = iter(range(64))
    due = {}
    sent = []

    def sems():
        i = next(sem_ids)
        return send_sems.at[i], recv_sems.at[i]

    def expect(name, ref, sem):
        due[name] = lambda: await_bytes(ref, sem)

    def settle(name):
        due.pop(name)()

    def leaves(ref, sem):
        sent.append(lambda: await_bytes(ref, sem))

    barrier = pltpu.get_barrier_semaphore()
    y_line = [device((y + d) % 8, core, x, z) for d in range(1, Y)]
    z_line = [device(y, core, x, (z + d) % 8) for d in range(1, Z)]
    x_line = [device(y, core, (x + d) % 4, z) for d in range(1, X)]
    for other in [partner] + x_line + y_line + z_line:
        pl.semaphore_signal(barrier, inc=1, device_id=other, device_id_type=MESH)

    loads = []
    for i, (src, dst) in enumerate(
        zip((send_hbm, feat_hbm, shard_hbm, nbr_hbm, degree_hbm, cot_hbm), (send_row, feat, shard, nbr_t, degree, cot))
    ):
        loads.append(pltpu.make_async_copy(src, dst, load_sems.at[i]))
        loads[i].start()

    loads[0].wait()
    own_id = lax.broadcasted_iota(I32, (NODES, 128), 0)
    for b in range(BOUND // 128):
        one_hot = jnp.where(own_id == send_row[:, b * 128 : (b + 1) * 128], 1.0, 0.0)
        pick_rows[b * 128 : (b + 1) * 128, :] = one_hot.T
    hub_pick = jnp.where(lax.broadcasted_iota(I32, (16, NODES), 1) == hub_at[0], 1.0, 0.0).astype(BF16)
    loads[1].wait()
    hub_wide = dot(hub_pick, feat[...])[0:8]
    lane_group = lax.broadcasted_iota(I32, (8, 128), 0)
    own_hub = jnp.zeros((8, 128), F32)
    for j in range(8):
        own_hub = jnp.where(lane_group == j, hub_wide[:, j * 128 : (j + 1) * 128], own_hub)
    hub_tile[...] = jnp.concatenate([own_hub, own_hub], axis=0).astype(BF16)
    loads[2].wait()
    pl.semaphore_wait(barrier, len(x_line) + len(y_line) + len(z_line) + 1)

    w_z, w_x, w_core = sems(), sems(), sems()
    half = pl.ds(pl.multiple_of(core * 16, 16), 16)
    for other in z_line:
        remote(shard.at[half], full_weight.at[x, z, core], w_z, other)
    expect("w_z", full_weight.at[0, pl.ds(0, 7), 0], w_z[1])
    leaves(full_weight.at[0, pl.ds(0, 7), 0], w_z[0])
    for other in y_line:
        pl.semaphore_signal(entered.at[0], inc=1, device_id=other, device_id_type=MESH)
    h_core, h_z, h_y, h_x, h_last = sems(), sems(), sems(), sems(), sems()
    remote(hub_tile, hub_other, h_core, partner)
    expect("h_core", hub_other, h_core[1])
    leaves(hub_tile, h_core[0])
    full_weight[x, z, 0] = shard[0:16]
    full_weight[x, z, 1] = shard[16:32]

    def in_tiles(ref, base, n, part):
        for e in range(2):
            ref[pl.ds(base + 2 * n + e, part.shape[0], stride=8), :] = part[:, e * 128 : (e + 1) * 128]

    def table_row(g, dx, i, which):
        row = ((y + g + i // 8 * 4) % 8) * 64 + which * 32 + (4 - dx) % 4 * 8 + (z + i) % 8
        return table[pl.ds(pl.multiple_of(row * 8, 8), 8), :]

    def swap_start(g, ends):
        swap_out, swap_in, pair = ends["swap_out"], ends["swap_in"], ends["swap"][g]
        for dx in range(X):

            def build(m, carry):
                rows = [table_row(g, dx, 2 * m + e, 1) for e in range(2)]
                swap_out[g * 32 + dx * 8 + m] = jnp.concatenate(rows, axis=0).astype(BF16)
                return carry

            lax.fori_loop(0, 8, build, 0, unroll=4)
        part = pl.ds(g * 32, 32)
        remote(swap_out.at[part], swap_in.at[part], pair, partner)
        expect(("swap", g), swap_in.at[part], pair[1])
        leaves(swap_out.at[part], pair[0])

    def along_x(g, ends):
        stage, mid = ends["stage"], ends["mid"]
        settle(("swap", g))
        for dx in (2, 1, 3, 0):

            def pair_up(m, carry):
                theirs = ends["swap_in"][g * 32 + dx * 8 + m].astype(F32)
                for e in range(2):
                    i = 2 * m + e
                    tile = jnp.concatenate([table_row(g, dx, i, 0), theirs[8 * e : 8 * e + 8]], axis=0)
                    stage[g, dx, i] = tile.astype(BF16)
                return carry

            lax.fori_loop(0, 8, pair_up, 0, unroll=4)
            if dx:
                remote(stage.at[g, dx], mid.at[g, dx - 1], ends["x"][g], x_line[dx - 1])
        expect(("x", g), mid.at[g], ends["x"][g][1])
        leaves(mid.at[g], ends["x"][g][0])

    def to_plane(g, ends, name, src, dst, tile_count):
        pair = ends[name][g]

        def post(i, carry):
            to = device((y + g + i // 8 * 4) % 8, core, x, (z + i) % 8)
            remote(src(i), dst, pair, to)
            return carry

        first = 0 if g else 1
        lax.fori_loop(first, 16, post, 0)
        same_size = tile_count(16 - first)
        expect((name, g), same_size, pair[1])
        leaves(same_size, pair[0])

    def post_own(g, ends):
        stage, came = ends["stage"], ends["came"]
        to_plane(
            g, ends, "own", lambda i: stage.at[g, 0, i], came.at[slot_y, 0, z], lambda n: stage.at[g, 0, pl.ds(0, n)]
        )
        if g == 0:
            came[slot_y, 0, z] = stage[0, 0, 0]

    def post_far(g, ends):
        mid, came = ends["mid"], ends["came"]
        settle(("x", g))
        to_plane(
            g, ends, "far", lambda i: mid.at[g, :, i], came.at[slot_y, pl.ds(1, 3), z], lambda n: mid.at[g, :, pl.ds(0, n)]
        )
        if g == 0:
            for d in range(3):
                came[slot_y, 1 + d, z] = mid[0, d, 0]

    def received(g, ends):
        came = ends["came"]
        settle(("own", g))
        settle(("far", g))
        from_y = (y + 4 - g) % 4
        for h in range(2):
            wide[h * 512 : (h + 1) * 512, :] = came[from_y * 2 + h].reshape(512, 128).astype(F32)

        def columns(n):
            sides = []
            for j in (2 * n, 2 * n + 1):
                parts = [wide[pl.ds(h * 512 + w * 8 + j, 32, stride=16), :] for h in range(2) for w in range(2)]
                sides.append(jnp.concatenate(parts, axis=0))
            return jnp.concatenate(sides, axis=1).astype(BF16)

        return from_y, columns

    def exchange_ends(swap_out, swap_in, stage, mid, came):
        ends = dict(swap_out=swap_out, swap_in=swap_in, stage=stage, mid=mid, came=came)
        for name in ("swap", "x", "own", "far"):
            ends[name] = [sems() for _ in GROUPS]
        return ends

    def to_table(base_y, n, part):
        for h in range(2):
            in_tiles(table, (h * 4 + base_y) * 512, n, part[h * 64 : (h + 1) * 64])

    ends_f = exchange_ends(swap_out_f, swap_in_f, stage_f, mid_f, came_f)

    def select(g):
        to_y = (y + g) % 4
        rows = []
        for h in range(2):
            for which in range(2):
                other = (core + which) % 2
                for q in range(X):
                    row = (h * 4 + to_y) * 64 + other * 32 + (x + 4 - q) % 4 * 8
                    rows.append(pick_rows[pl.ds(pl.multiple_of(row, 8), 8), :])
        chosen = jnp.concatenate(rows, axis=0)
        picks[to_y] = chosen.T.astype(BF16)
        chosen = chosen.astype(BF16)
        for n in range(4):
            to_table(to_y, n, dot(chosen, feat[:, block(n)]))

    g0, g1, g2, g3 = GROUPS
    select(g0)
    swap_start(g0, ends_f)

    settle("h_core")
    theirs = hub_other[...].astype(F32)[0:8]
    first = jnp.where(core == 0, own_hub, theirs)
    second = jnp.where(core == 0, theirs, own_hub)
    z_slab = ((x * 2 + core) * 8 + y) * 4

    @pl.when(holds)
    def _():
        slot = z_slab + z % 4
        hub_tiles[slot] = jnp.concatenate([first, second], axis=0).astype(BF16)
        for other in z_line:
            remote(hub_tiles.at[slot], hub_tiles.at[slot], h_z, other)

    def hub_z_due():
        @pl.when(holds)
        def _():
            await_bytes(hub_tiles.at[pl.ds(0, 3)], h_z[1])

        @pl.when(jnp.logical_not(holds))
        def _():
            await_bytes(hub_tiles.at[pl.ds(0, 4)], h_z[1])

    def hub_z_left():
        @pl.when(holds)
        def _():
            await_bytes(hub_tiles.at[pl.ds(0, 7)], h_z[0])

    due["h_z"] = hub_z_due
    sent.append(hub_z_left)
    pl.semaphore_wait(entered.at[0], Y - 1)
    for other in z_line:
        pl.semaphore_signal(entered.at[1], inc=1, device_id=other, device_id_type=MESH)
    select(g1)
    along_x(g0, ends_f)
    swap_start(g1, ends_f)
    pl.semaphore_wait(entered.at[1], Z - 1)
    post_own(g0, ends_f)
    select(g2)
    along_x(g1, ends_f)
    post_own(g1, ends_f)
    swap_start(g2, ends_f)
    select(g3)
    along_x(g2, ends_f)
    post_far(g0, ends_f)
    post_own(g2, ends_f)
    swap_start(g3, ends_f)

    settle("h_z")
    y_slab = pl.ds(z_slab, 4)
    for other in y_line:
        remote(hub_tiles.at[y_slab], hub_tiles.at[y_slab], h_y, other)
    expect("h_y", hub_tiles.at[pl.ds(0, 28)], h_y[1])
    leaves(hub_tiles.at[pl.ds(0, 28)], h_y[0])
    along_x(g3, ends_f)

    settle("w_z")
    for other in x_line:
        remote(full_weight.at[x, :, core], full_weight.at[x, :, core], w_x, other)
    expect("w_x", full_weight.at[pl.ds(0, 3), :, 0], w_x[1])
    leaves(full_weight.at[pl.ds(0, 3), :, 0], w_x[0])
    post_far(g1, ends_f)
    post_own(g3, ends_f)
    post_far(g2, ends_f)

    settle("h_y")
    x_slab = pl.ds((x * 2 + core) * 32, 32)
    for other in x_line:
        remote(hub_tiles.at[x_slab], hub_tiles.at[x_slab], h_x, other)
    expect("h_x", hub_tiles.at[pl.ds(0, 96)], h_x[1])
    leaves(hub_tiles.at[pl.ds(0, 96)], h_x[0])
    post_far(g3, ends_f)

    loads[3].wait()
    loads[4].wait()
    number = nbr_t[...]
    s = number - NODES
    bound_column = (
        NODES + ((s >> 6) & 3) * 128 + (s >> 8) * 64 + (((s >> 5) + core) & 1) * 32
        + ((x - (s >> 3)) & 3) * 8 + (s & 7)
    )
    h = number - (NODES + BOUND)
    hub_column = (
        NODES + BOUND
        + ((((h >> 3) & 3) * 2 + ((h >> 2) & 1)) * 32 + (h >> 6) * 4 + (h & 3)) * 2
        + ((h >> 5) & 1)
    )
    column = jnp.where(number < NODES, number, jnp.where(number < NODES + BOUND, bound_column, hub_column))
    slot_id = lax.broadcasted_iota(I32, number.shape, 0)
    live = jnp.where(slot_id < degree[...], column, -1)
    for b in range(COLUMNS // 128):
        row_id = own_id + b * 128
        count = jnp.zeros((128, 128), F32)
        for k in range(live.shape[0]):
            count = count + jnp.where(live[k : k + 1, :] == row_id, 1.0, 0.0)
        edges_t[b * 128 : (b + 1) * 128, :] = count.astype(BF16)
        edges[:, b * 128 : (b + 1) * 128] = count.T.astype(BF16)
    div[...] = jnp.broadcast_to((degree[...] + 1).astype(F32), (128, 128)).T
    for n in range(4):
        rows = feat[:, block(n)]
        total[:, block(n)] = rows.astype(F32) + dot(edges[:, 0:NODES], rows)

    settle("h_x")
    for at in range(X):
        slab = pl.ds((at * 2 + core) * 32, 32)
        remote(hub_tiles.at[slab], hub_tiles.at[slab], h_last, partner)
    expect("h_last", hub_tiles.at[pl.ds(0, 128)], h_last[1])
    leaves(hub_tiles.at[pl.ds(0, 128)], h_last[0])
    settle("w_x")
    remote(full_weight.at[:, :, core], full_weight.at[:, :, core], w_core, partner)
    expect("w_core", full_weight.at[:, :, 0], w_core[1])
    leaves(full_weight.at[:, :, 0], w_core[0])

    settle("h_last")
    for part in range(8):
        hub_table[part * 512 : (part + 1) * 512, :] = (
            hub_tiles[part * 32 : (part + 1) * 32].reshape(512, 128).astype(F32)
        )
    for j in range(8):
        hub_lookup[:, j * 128 : (j + 1) * 128] = hub_table[pl.ds(j, HUBS, stride=8), :].astype(BF16)
    for n in range(4):
        total[:, block(n)] += dot(edges[:, NODES + BOUND : COLUMNS], hub_lookup[:, block(n)])

    for g in GROUPS:
        from_y, rows = received(g, ends_f)
        part = edges[:, pl.ds(pl.multiple_of(NODES + from_y * 128, 128), 128)]
        for n in range(4):
            total[:, block(n)] += dot(part, rows(n))

    settle("w_core")
    loads[5].wait()
    two_div = jnp.concatenate([div[...], div[...]], axis=1)
    for n in range(4):
        mean[:, block(n)] = (total[:, block(n)] / two_div).astype(BF16)
    for n in range(4):
        pre_act = jnp.zeros((NODES, 256), F32)
        for k in range(X):
            pre_act = pre_act + dot(mean[:, block(k)], full_weight[k, :, :, :, block(n)].reshape(256, 256))
        sig = jax.nn.sigmoid(pre_act)
        out[:, block(n)] = (pre_act * sig).astype(BF16)
        slope = sig * (1.0 + pre_act * (1.0 - sig))
        act[:, block(n)] = (cot[:, block(n)].astype(F32) * slope).astype(BF16)
    for n in range(X):
        term = lax.dot_general(
            act[...], full_weight[n].reshape(256, WIDTH), (((1,), (1,)), ((), ())), preferred_element_type=F32
        ) / two_div
        top = term.astype(BF16)
        terms[:, block(n)] = term
        high[:, block(n)] = top
        low[:, block(n)] = (term - top.astype(F32)).astype(BF16)

    def spread(rows, put):
        edge = edges_t[rows, :]
        for n in range(4):
            put(n, dot(edge, high[:, block(n)]) + dot(edge, low[:, block(n)]))

    ends_b = exchange_ends(swap_out_b, swap_in_b, stage_b, mid_b, came_b)
    g_core, g_x, g_y, g_z, g_last = sems(), sems(), sems(), sems(), sems()

    def give_back(g):
        to_y = (y + g) % 4
        spread(
            pl.ds(pl.multiple_of(NODES + to_y * 128, 128), 128), lambda n, part: to_table(to_y, n, part)
        )
        swap_start(g, ends_b)

    give_back(g0)

    spread(slice(NODES + BOUND, COLUMNS), lambda n, part: in_tiles(hub_table, 0, n, part))
    for at in range(X):
        slab = pl.ds(pl.multiple_of((at * 2 + 1 - core) * 512, 512), 512)
        remote(hub_table.at[slab], hub_core.at[at], g_core, partner)
    expect("g_core", hub_core, g_core[1])
    leaves(hub_core, g_core[0])
    along_x(g0, ends_b)
    post_own(g0, ends_b)
    give_back(g1)
    along_x(g1, ends_b)
    post_own(g1, ends_b)

    def kept(at):
        return hub_table[pl.ds(pl.multiple_of((at * 2 + core) * 512, 512), 512), :] + hub_core[at]

    settle("g_core")
    for d in range(1, X):
        hub_x_out[d - 1] = kept((x + d) % 4).astype(BF16)
        remote(hub_x_out.at[d - 1], hub_x_in.at[d - 1], g_x, x_line[d - 1])
    expect("g_x", hub_x_in, g_x[1])
    leaves(hub_x_in, g_x[0])
    post_far(g0, ends_b)
    give_back(g2)
    along_x(g2, ends_b)
    post_own(g2, ends_b)
    post_far(g1, ends_b)
    give_back(g3)
    along_x(g3, ends_b)
    post_own(g3, ends_b)

    settle("g_x")
    part = kept(x)
    for d in range(X - 1):
        part = part + hub_x_in[d].astype(F32)
    hub_x_sum[...] = part
    hub_y_out[...] = part.astype(BF16).reshape(Y, 64, 128)
    for d in range(1, Y):
        remote(hub_y_out.at[(y + d) % 8], hub_y_in.at[d - 1], g_y, y_line[d - 1])
    expect("g_y", hub_y_in, g_y[1])
    leaves(hub_y_in, g_y[0])
    post_far(g2, ends_b)
    post_far(g3, ends_b)

    for n in range(4):
        cols = block(n)
        own_sum[:, cols] = terms[:, cols] + dot(edges_t[0:NODES, :], high[:, cols]) + dot(edges_t[0:NODES, :], low[:, cols])
    settle("g_y")
    part = hub_x_sum[pl.ds(pl.multiple_of(y * 64, 64), 64), :]
    for d in range(Y - 1):
        part = part + hub_y_in[d].astype(F32)
    hub_y_sum[...] = part
    for at in range(4):
        to = core * 4 + at

        @pl.when(to != z)
        def _():
            slot = (to - z + 8) % 8 - 1
            remote(hub_y_sum.at[pl.ds(at * 16, 16)], hub_z_in.at[slot], g_z, device(y, core, x, to))

    for g in (g0, g1):
        from_y, rows = received(g, ends_b)
        for n in range(4):
            own_sum[:, block(n)] += dot(picks[from_y], rows(n))

    @pl.when(holds)
    def _():
        await_bytes(hub_z_in, g_z[1])
        here = hub_y_sum[pl.ds(pl.multiple_of((z % 4) * 16, 16), 16), :]
        for d in range(Z - 1):
            here = here + hub_z_in[d]
        hub_z_sum[...] = here
        remote(hub_z_sum, hub_last, g_last, partner)
        hub_row[...] = hub_z_sum[pl.ds(pl.multiple_of(core * 8, 8), 8), :]
        await_bytes(hub_z_in.at[pl.ds(0, 3)], g_z[0])
        await_bytes(hub_z_sum, g_last[0])

    @pl.when(jnp.logical_not(holds))
    def _():
        await_bytes(hub_last, g_last[1])
        hub_row[...] = hub_last[pl.ds(pl.multiple_of(core * 8, 8), 8), :]
        await_bytes(hub_z_in.at[pl.ds(0, 4)], g_z[0])

    hub_mask = own_id == hub_at[0]
    for j in range(8):
        cols = slice(j * 128, (j + 1) * 128)
        own_sum[:, cols] += jnp.where(hub_mask, hub_row[j : j + 1, :], 0.0)

    from_y, rows = received(g2, ends_b)
    for n in range(4):
        own_sum[:, block(n)] += dot(picks[from_y], rows(n))
    from_y, rows = received(g3, ends_b)
    for n in range(4):
        grad[:, block(n)] = (own_sum[:, block(n)] + dot(picks[from_y], rows(n))).astype(BF16)
    for wait in sent:
        wait()


def tiles(count):
    return pltpu.VMEM((count, 16, 128), BF16)


ENDS = [
    tiles(128),
    tiles(128),
    pltpu.VMEM((4, X, 16, 16, 128), BF16),
    pltpu.VMEM((4, X - 1, 16, 16, 128), BF16),
    pltpu.VMEM((Y, X, Z, 16, 128), BF16),
]

SCRATCH = [
    pltpu.VMEM((NODES, WIDTH), BF16),
    pltpu.VMEM((NODES, WIDTH), BF16),
    pltpu.VMEM((32, WIDTH), BF16),
    pltpu.VMEM((16, NODES), I32),
    pltpu.VMEM((1, NODES), I32),
    pltpu.VMEM((1, BOUND), I32),
    pltpu.VMEM((BOUND, NODES), F32),
    pltpu.VMEM((X, NODES, 128), BF16),
    pltpu.VMEM((4096, 128), F32),
    pltpu.VMEM((1024, 128), F32),
    pltpu.VMEM((X, Z, 2, 16, WIDTH), BF16),
    pltpu.VMEM((NODES, COLUMNS), BF16),
    pltpu.VMEM((COLUMNS, NODES), BF16),
    pltpu.VMEM((HUBS, WIDTH), BF16),
    pltpu.VMEM((128, 128), F32),
    pltpu.VMEM((NODES, WIDTH), F32),
    pltpu.VMEM((NODES, WIDTH), BF16),
    pltpu.VMEM((NODES, WIDTH), BF16),
    pltpu.VMEM((NODES, WIDTH), F32),
    pltpu.VMEM((NODES, WIDTH), BF16),
    pltpu.VMEM((NODES, WIDTH), BF16),
    pltpu.VMEM((NODES, WIDTH), F32),
    *ENDS,
    *ENDS,
    pltpu.VMEM((16, 128), BF16),
    pltpu.VMEM((16, 128), BF16),
    tiles(256),
    pltpu.VMEM((4096, 128), F32),
    pltpu.VMEM((X, 512, 128), F32),
    pltpu.VMEM((X - 1, 512, 128), BF16),
    pltpu.VMEM((X - 1, 512, 128), BF16),
    pltpu.VMEM((512, 128), F32),
    pltpu.VMEM((Y, 64, 128), BF16),
    pltpu.VMEM((Y - 1, 64, 128), BF16),
    pltpu.VMEM((64, 128), F32),
    pltpu.VMEM((Z - 1, 16, 128), F32),
    pltpu.VMEM((16, 128), F32),
    pltpu.VMEM((16, 128), F32),
    pltpu.VMEM((8, 128), F32),
    pltpu.SemaphoreType.DMA((48,)),
    pltpu.SemaphoreType.DMA((48,)),
    pltpu.SemaphoreType.DMA((6,)),
    pltpu.SemaphoreType.REGULAR((2,)),
]


def on_device(feat, cotangent, weight, nbr_index, degree, send_rows, hub_rows):
    vmem = pl.BlockSpec(memory_space=pltpu.VMEM)
    hbm = pl.BlockSpec(memory_space=pltpu.HBM)
    smem = pl.BlockSpec(memory_space=pltpu.SMEM)
    return pl.pallas_call(
        whole_kernel,
        out_shape=(
            jax.ShapeDtypeStruct((NODES, WIDTH), BF16),
            jax.ShapeDtypeStruct((NODES, WIDTH), BF16),
        ),
        in_specs=[hbm] * 6 + [smem],
        out_specs=(vmem, vmem),
        scratch_shapes=SCRATCH,
        compiler_params=pltpu.CompilerParams(has_side_effects=True, collective_id=0, vmem_limit_bytes=63 << 20),
        name="sage",
    )(feat, cotangent, weight, nbr_index.T, degree[None, :], send_rows.T, hub_rows)


def solution(mesh):
    placed = (
        P(("region", "sub"), None),
        P(("region", "sub"), None),
        P("sub", None),
        P(("region", "sub"), None),
        P(("region", "sub")),
        P(("region", "sub"), None),
        P(("region", "sub")),
    )
    return jax.shard_map(
        on_device,
        mesh=mesh,
        in_specs=placed,
        out_specs=(P(("region", "sub"), None), P(("region", "sub"), None)),
        check_vma=False,
    )
```

```python
import jax
import jax.numpy as jnp
from jax import lax
from jax.experimental import pallas as pl
from jax.experimental.pallas import tpu as pltpu
from jax.sharding import PartitionSpec as P

MESH = pl.DeviceIdType.MESH
BF16, F32, I32 = jnp.bfloat16, jnp.float32, jnp.int32
Y, X, Z = 8, 4, 8
NODES, WIDTH, BOUND, HUBS = 128, 1024, 512, 512
COLUMNS = NODES + BOUND + HUBS
GROUPS = (2, 1, 3, 0)


def place():
    region = lax.axis_index("region")
    sub = lax.axis_index("sub")
    return region // 2, region % 2, sub // 8, sub % 8


def device(y, core, x, z):
    return (y * 2 + core, x * 8 + z)


def remote(src, dst, sems, target):
    pltpu.make_async_remote_copy(
        src_ref=src, dst_ref=dst, send_sem=sems[0], recv_sem=sems[1], device_id=target, device_id_type=MESH
    ).start()


def await_bytes(ref, sem):
    pltpu.make_async_copy(ref, ref, sem).wait()


def dot(a, b):
    return jnp.dot(a, b, preferred_element_type=F32)


def block(n):
    return slice(n * 256, (n + 1) * 256)


def whole_kernel(
    feat_hbm, cot_hbm, shard_hbm, nbr_hbm, degree_hbm, send_hbm, hub_at,
    out, grad,
    feat, cot, shard, nbr_t, degree, send_row,
    pick_rows, picks, table, wide, full_weight, edges, edges_t, hub_lookup, div, total, mean, act, terms, high, low, own_sum,
    swap_out_f, swap_in_f, stage_f, mid_f, came_f, swap_out_b, swap_in_b, stage_b, mid_b, came_b,
    hub_tile, hub_other, hub_tiles, hub_table,
    hub_core, hub_x_out, hub_x_in, hub_x_sum, hub_y_out, hub_y_in, hub_y_sum, hub_z_in, hub_z_sum, hub_last, hub_row,
    send_sems, recv_sems, load_sems, entered,
):
    y, core, x, z = place()
    slot_y = (y % 4) * 2 + y // 4
    partner = device(y, 1 - core, x, z)
    holds = core == z // 4
    sem_ids = iter(range(64))
    due = {}
    sent = []

    def sems():
        i = next(sem_ids)
        return send_sems.at[i], recv_sems.at[i]

    def expect(name, ref, sem):
        due[name] = lambda: await_bytes(ref, sem)

    def settle(name):
        due.pop(name)()

    def leaves(ref, sem):
        sent.append(lambda: await_bytes(ref, sem))

    barrier = pltpu.get_barrier_semaphore()
    y_line = [device((y + d) % 8, core, x, z) for d in range(1, Y)]
    z_line = [device(y, core, x, (z + d) % 8) for d in range(1, Z)]
    x_line = [device(y, core, (x + d) % 4, z) for d in range(1, X)]
    for other in [partner] + x_line + y_line + z_line:
        pl.semaphore_signal(barrier, inc=1, device_id=other, device_id_type=MESH)

    loads = []
    for i, (src, dst) in enumerate(
        zip((send_hbm, feat_hbm, shard_hbm, nbr_hbm, degree_hbm, cot_hbm), (send_row, feat, shard, nbr_t, degree, cot))
    ):
        loads.append(pltpu.make_async_copy(src, dst, load_sems.at[i]))
        loads[i].start()

    loads[0].wait()
    own_id = lax.broadcasted_iota(I32, (NODES, 128), 0)
    for b in range(BOUND // 128):
        one_hot = jnp.where(own_id == send_row[:, b * 128 : (b + 1) * 128], 1.0, 0.0)
        pick_rows[b * 128 : (b + 1) * 128, :] = one_hot.T
    hub_pick = jnp.where(lax.broadcasted_iota(I32, (16, NODES), 1) == hub_at[0], 1.0, 0.0).astype(BF16)
    loads[1].wait()
    hub_wide = dot(hub_pick, feat[...])[0:8]
    lane_group = lax.broadcasted_iota(I32, (8, 128), 0)
    own_hub = jnp.zeros((8, 128), F32)
    for j in range(8):
        own_hub = jnp.where(lane_group == j, hub_wide[:, j * 128 : (j + 1) * 128], own_hub)
    hub_tile[...] = jnp.concatenate([own_hub, own_hub], axis=0).astype(BF16)
    def in_tiles(ref, base, n, part):
        for e in range(2):
            ref[pl.ds(base + 2 * n + e, part.shape[0], stride=8), :] = part[:, e * 128 : (e + 1) * 128]

    def table_row(g, dx, i, which):
        row = ((y + g + i // 8 * 4) % 8) * 64 + which * 32 + (4 - dx) % 4 * 8 + (z + i) % 8
        return table[pl.ds(pl.multiple_of(row * 8, 8), 8), :]

    def swap_build(g, ends):
        swap_out = ends["swap_out"]
        for dx in range(X):

            def build(m, carry):
                rows = [table_row(g, dx, 2 * m + e, 1) for e in range(2)]
                swap_out[g * 32 + dx * 8 + m] = jnp.concatenate(rows, axis=0).astype(BF16)
                return carry

            lax.fori_loop(0, 8, build, 0, unroll=4)

    def swap_send(g, ends):
        swap_out, swap_in, pair = ends["swap_out"], ends["swap_in"], ends["swap"][g]
        part = pl.ds(g * 32, 32)
        remote(swap_out.at[part], swap_in.at[part], pair, partner)
        expect(("swap", g), swap_in.at[part], pair[1])
        leaves(swap_out.at[part], pair[0])

    def along_x(g, ends):
        stage, mid = ends["stage"], ends["mid"]
        settle(("swap", g))
        for dx in (2, 1, 3, 0):

            def pair_up(m, carry):
                theirs = ends["swap_in"][g * 32 + dx * 8 + m].astype(F32)
                for e in range(2):
                    i = 2 * m + e
                    tile = jnp.concatenate([table_row(g, dx, i, 0), theirs[8 * e : 8 * e + 8]], axis=0)
                    stage[g, dx, i] = tile.astype(BF16)
                return carry

            lax.fori_loop(0, 8, pair_up, 0, unroll=4)
            if dx:
                remote(stage.at[g, dx], mid.at[g, dx - 1], ends["x"][g], x_line[dx - 1])
        expect(("x", g), mid.at[g], ends["x"][g][1])
        leaves(mid.at[g], ends["x"][g][0])

    def to_plane(g, ends, name, src, dst, tile_count):
        pair = ends[name][g]

        def post(i, carry):
            to = device((y + g + i // 8 * 4) % 8, core, x, (z + i) % 8)
            remote(src(i), dst, pair, to)
            return carry

        first = 0 if g else 1
        lax.fori_loop(first, 16, post, 0)
        same_size = tile_count(16 - first)
        expect((name, g), same_size, pair[1])
        leaves(same_size, pair[0])

    def post_own(g, ends):
        stage, came = ends["stage"], ends["came"]
        to_plane(
            g, ends, "own", lambda i: stage.at[g, 0, i], came.at[slot_y, 0, z], lambda n: stage.at[g, 0, pl.ds(0, n)]
        )
        if g == 0:
            came[slot_y, 0, z] = stage[0, 0, 0]

    def post_far(g, ends):
        mid, came = ends["mid"], ends["came"]
        settle(("x", g))
        to_plane(
            g, ends, "far", lambda i: mid.at[g, :, i], came.at[slot_y, pl.ds(1, 3), z], lambda n: mid.at[g, :, pl.ds(0, n)]
        )
        if g == 0:
            for d in range(3):
                came[slot_y, 1 + d, z] = mid[0, d, 0]

    def received(g, ends):
        came = ends["came"]
        settle(("own", g))
        settle(("far", g))
        from_y = (y + 4 - g) % 4
        for h in range(2):
            wide[h * 512 : (h + 1) * 512, :] = came[from_y * 2 + h].reshape(512, 128).astype(F32)

        def columns(n):
            sides = []
            for j in (2 * n, 2 * n + 1):
                parts = [wide[pl.ds(h * 512 + w * 8 + j, 32, stride=16), :] for h in range(2) for w in range(2)]
                sides.append(jnp.concatenate(parts, axis=0))
            return jnp.concatenate(sides, axis=1).astype(BF16)

        return from_y, columns

    def exchange_ends(swap_out, swap_in, stage, mid, came):
        ends = dict(swap_out=swap_out, swap_in=swap_in, stage=stage, mid=mid, came=came)
        for name in ("swap", "x", "own", "far"):
            ends[name] = [sems() for _ in GROUPS]
        return ends

    def to_table(base_y, n, part):
        for h in range(2):
            in_tiles(table, (h * 4 + base_y) * 512, n, part[h * 64 : (h + 1) * 64])

    ends_f = exchange_ends(swap_out_f, swap_in_f, stage_f, mid_f, came_f)

    def select(g):
        to_y = (y + g) % 4
        rows = []
        for h in range(2):
            for which in range(2):
                other = (core + which) % 2
                for q in range(X):
                    row = (h * 4 + to_y) * 64 + other * 32 + (x + 4 - q) % 4 * 8
                    rows.append(pick_rows[pl.ds(pl.multiple_of(row, 8), 8), :])
        chosen = jnp.concatenate(rows, axis=0)
        picks[to_y] = chosen.T.astype(BF16)
        chosen = chosen.astype(BF16)
        for n in range(4):
            to_table(to_y, n, dot(chosen, feat[:, block(n)]))

    g0, g1, g2, g3 = GROUPS
    select(g0)
    swap_build(g0, ends_f)
    select(g1)
    loads[2].wait()
    pl.semaphore_wait(barrier, len(x_line) + len(y_line) + len(z_line) + 1)
    for d in range(1, Y):
        pl.semaphore_signal(entered.at[Y - d], inc=1, device_id=y_line[d - 1], device_id_type=MESH)
    swap_send(g0, ends_f)

    w_z, w_x, w_core = sems(), sems(), sems()
    half = pl.ds(pl.multiple_of(core * 16, 16), 16)
    for other in z_line:
        remote(shard.at[half], full_weight.at[x, z, core], w_z, other)
    expect("w_z", full_weight.at[0, pl.ds(0, 7), 0], w_z[1])
    leaves(full_weight.at[0, pl.ds(0, 7), 0], w_z[0])
    h_core, h_z, h_y, h_x, h_last = sems(), sems(), sems(), sems(), sems()
    remote(hub_tile, hub_other, h_core, partner)
    expect("h_core", hub_other, h_core[1])
    leaves(hub_tile, h_core[0])
    full_weight[x, z, 0] = shard[0:16]
    full_weight[x, z, 1] = shard[16:32]

    settle("h_core")
    theirs = hub_other[...].astype(F32)[0:8]
    first = jnp.where(core == 0, own_hub, theirs)
    second = jnp.where(core == 0, theirs, own_hub)
    z_slab = ((x * 2 + core) * 8 + y) * 4

    @pl.when(holds)
    def _():
        slot = z_slab + z % 4
        hub_tiles[slot] = jnp.concatenate([first, second], axis=0).astype(BF16)
        for other in z_line:
            remote(hub_tiles.at[slot], hub_tiles.at[slot], h_z, other)

    def hub_z_due():
        @pl.when(holds)
        def _():
            await_bytes(hub_tiles.at[pl.ds(0, 3)], h_z[1])

        @pl.when(jnp.logical_not(holds))
        def _():
            await_bytes(hub_tiles.at[pl.ds(0, 4)], h_z[1])

    def hub_z_left():
        @pl.when(holds)
        def _():
            await_bytes(hub_tiles.at[pl.ds(0, 7)], h_z[0])

    due["h_z"] = hub_z_due
    sent.append(hub_z_left)
    along_x(g0, ends_f)
    swap_build(g1, ends_f)
    swap_send(g1, ends_f)

    def greeted(g):
        for dy in (g, g + 4):
            if dy:
                pl.semaphore_wait(entered.at[dy], 1)

    greeted(g0)
    post_own(g0, ends_f)
    select(g2)
    along_x(g1, ends_f)
    greeted(g1)
    post_own(g1, ends_f)
    swap_build(g2, ends_f)
    swap_send(g2, ends_f)
    select(g3)
    along_x(g2, ends_f)
    post_far(g0, ends_f)
    greeted(g2)
    post_own(g2, ends_f)
    swap_build(g3, ends_f)
    swap_send(g3, ends_f)

    settle("h_z")
    y_slab = pl.ds(z_slab, 4)
    for other in y_line:
        remote(hub_tiles.at[y_slab], hub_tiles.at[y_slab], h_y, other)
    expect("h_y", hub_tiles.at[pl.ds(0, 28)], h_y[1])
    leaves(hub_tiles.at[pl.ds(0, 28)], h_y[0])
    along_x(g3, ends_f)

    settle("w_z")
    for other in x_line:
        remote(full_weight.at[x, :, core], full_weight.at[x, :, core], w_x, other)
    expect("w_x", full_weight.at[pl.ds(0, 3), :, 0], w_x[1])
    leaves(full_weight.at[pl.ds(0, 3), :, 0], w_x[0])
    post_far(g1, ends_f)
    greeted(g3)
    post_own(g3, ends_f)
    post_far(g2, ends_f)

    settle("h_y")
    x_slab = pl.ds((x * 2 + core) * 32, 32)
    for other in x_line:
        remote(hub_tiles.at[x_slab], hub_tiles.at[x_slab], h_x, other)
    expect("h_x", hub_tiles.at[pl.ds(0, 96)], h_x[1])
    leaves(hub_tiles.at[pl.ds(0, 96)], h_x[0])
    post_far(g3, ends_f)

    loads[3].wait()
    loads[4].wait()
    number = nbr_t[...]
    s = number - NODES
    bound_column = (
        NODES + ((s >> 6) & 3) * 128 + (s >> 8) * 64 + (((s >> 5) + core) & 1) * 32
        + ((x - (s >> 3)) & 3) * 8 + (s & 7)
    )
    h = number - (NODES + BOUND)
    hub_column = (
        NODES + BOUND
        + ((((h >> 3) & 3) * 2 + ((h >> 2) & 1)) * 32 + (h >> 6) * 4 + (h & 3)) * 2
        + ((h >> 5) & 1)
    )
    column = jnp.where(number < NODES, number, jnp.where(number < NODES + BOUND, bound_column, hub_column))
    slot_id = lax.broadcasted_iota(I32, number.shape, 0)
    live = jnp.where(slot_id < degree[...], column, -1)
    for b in range(COLUMNS // 128):
        row_id = own_id + b * 128
        count = jnp.zeros((128, 128), F32)
        for k in range(live.shape[0]):
            count = count + jnp.where(live[k : k + 1, :] == row_id, 1.0, 0.0)
        edges_t[b * 128 : (b + 1) * 128, :] = count.astype(BF16)
        edges[:, b * 128 : (b + 1) * 128] = count.T.astype(BF16)
    div[...] = jnp.broadcast_to((degree[...] + 1).astype(F32), (128, 128)).T
    for n in range(4):
        rows = feat[:, block(n)]
        total[:, block(n)] = rows.astype(F32) + dot(edges[:, 0:NODES], rows)

    settle("h_x")
    for at in range(X):
        slab = pl.ds((at * 2 + core) * 32, 32)
        remote(hub_tiles.at[slab], hub_tiles.at[slab], h_last, partner)
    expect("h_last", hub_tiles.at[pl.ds(0, 128)], h_last[1])
    leaves(hub_tiles.at[pl.ds(0, 128)], h_last[0])
    settle("w_x")
    remote(full_weight.at[:, :, core], full_weight.at[:, :, core], w_core, partner)
    expect("w_core", full_weight.at[:, :, 0], w_core[1])
    leaves(full_weight.at[:, :, 0], w_core[0])

    settle("h_last")
    for part in range(8):
        hub_table[part * 512 : (part + 1) * 512, :] = (
            hub_tiles[part * 32 : (part + 1) * 32].reshape(512, 128).astype(F32)
        )
    for j in range(8):
        hub_lookup[:, j * 128 : (j + 1) * 128] = hub_table[pl.ds(j, HUBS, stride=8), :].astype(BF16)
    for n in range(4):
        total[:, block(n)] += dot(edges[:, NODES + BOUND : COLUMNS], hub_lookup[:, block(n)])

    for g in GROUPS:
        from_y, rows = received(g, ends_f)
        part = edges[:, pl.ds(pl.multiple_of(NODES + from_y * 128, 128), 128)]
        for n in range(4):
            total[:, block(n)] += dot(part, rows(n))

    settle("w_core")
    loads[5].wait()
    two_div = jnp.concatenate([div[...], div[...]], axis=1)
    for n in range(4):
        mean[:, block(n)] = (total[:, block(n)] / two_div).astype(BF16)
    for n in range(4):
        pre_act = jnp.zeros((NODES, 256), F32)
        for k in range(X):
            pre_act = pre_act + dot(mean[:, block(k)], full_weight[k, :, :, :, block(n)].reshape(256, 256))
        sig = jax.nn.sigmoid(pre_act)
        out[:, block(n)] = (pre_act * sig).astype(BF16)
        slope = sig * (1.0 + pre_act * (1.0 - sig))
        act[:, block(n)] = (cot[:, block(n)].astype(F32) * slope).astype(BF16)
    for n in range(X):
        term = lax.dot_general(
            act[...], full_weight[n].reshape(256, WIDTH), (((1,), (1,)), ((), ())), preferred_element_type=F32
        ) / two_div
        top = term.astype(BF16)
        terms[:, block(n)] = term
        high[:, block(n)] = top
        low[:, block(n)] = (term - top.astype(F32)).astype(BF16)

    def spread(rows, put):
        edge = edges_t[rows, :]
        for n in range(4):
            put(n, dot(edge, high[:, block(n)]) + dot(edge, low[:, block(n)]))

    ends_b = exchange_ends(swap_out_b, swap_in_b, stage_b, mid_b, came_b)
    g_core, g_x, g_y, g_z, g_last = sems(), sems(), sems(), sems(), sems()

    def give_back(g):
        to_y = (y + g) % 4
        spread(
            pl.ds(pl.multiple_of(NODES + to_y * 128, 128), 128), lambda n, part: to_table(to_y, n, part)
        )
        swap_build(g, ends_b)
        swap_send(g, ends_b)

    give_back(g0)

    give_back(g1)
    along_x(g0, ends_b)
    post_own(g0, ends_b)

    spread(slice(NODES + BOUND, COLUMNS), lambda n, part: in_tiles(hub_table, 0, n, part))
    for at in range(X):
        slab = pl.ds(pl.multiple_of((at * 2 + 1 - core) * 512, 512), 512)
        remote(hub_table.at[slab], hub_core.at[at], g_core, partner)
    expect("g_core", hub_core, g_core[1])
    leaves(hub_core, g_core[0])
    along_x(g1, ends_b)
    post_own(g1, ends_b)
    give_back(g2)

    def kept(at):
        return hub_table[pl.ds(pl.multiple_of((at * 2 + core) * 512, 512), 512), :] + hub_core[at]

    settle("g_core")
    for d in range(1, X):
        hub_x_out[d - 1] = kept((x + d) % 4).astype(BF16)
        remote(hub_x_out.at[d - 1], hub_x_in.at[d - 1], g_x, x_line[d - 1])
    expect("g_x", hub_x_in, g_x[1])
    leaves(hub_x_in, g_x[0])
    post_far(g0, ends_b)
    along_x(g2, ends_b)
    post_own(g2, ends_b)
    give_back(g3)
    post_far(g1, ends_b)
    along_x(g3, ends_b)
    post_own(g3, ends_b)

    settle("g_x")
    part = kept(x)
    for d in range(X - 1):
        part = part + hub_x_in[d].astype(F32)
    hub_x_sum[...] = part
    hub_y_out[...] = part.astype(BF16).reshape(Y, 64, 128)
    for d in range(1, Y):
        remote(hub_y_out.at[(y + d) % 8], hub_y_in.at[d - 1], g_y, y_line[d - 1])
    expect("g_y", hub_y_in, g_y[1])
    leaves(hub_y_in, g_y[0])
    post_far(g2, ends_b)
    post_far(g3, ends_b)

    for n in range(4):
        cols = block(n)
        own_sum[:, cols] = terms[:, cols] + dot(edges_t[0:NODES, :], high[:, cols]) + dot(edges_t[0:NODES, :], low[:, cols])
    settle("g_y")
    part = hub_x_sum[pl.ds(pl.multiple_of(y * 64, 64), 64), :]
    for d in range(Y - 1):
        part = part + hub_y_in[d].astype(F32)
    hub_y_sum[...] = part
    for at in range(4):
        to = core * 4 + at

        @pl.when(to != z)
        def _():
            slot = (to - z + 8) % 8 - 1
            remote(hub_y_sum.at[pl.ds(at * 16, 16)], hub_z_in.at[slot], g_z, device(y, core, x, to))

    for g in (g0, g1):
        from_y, rows = received(g, ends_b)
        for n in range(4):
            own_sum[:, block(n)] += dot(picks[from_y], rows(n))

    @pl.when(holds)
    def _():
        await_bytes(hub_z_in, g_z[1])
        here = hub_y_sum[pl.ds(pl.multiple_of((z % 4) * 16, 16), 16), :]
        for d in range(Z - 1):
            here = here + hub_z_in[d]
        hub_z_sum[...] = here
        remote(hub_z_sum, hub_last, g_last, partner)
        hub_row[...] = hub_z_sum[pl.ds(pl.multiple_of(core * 8, 8), 8), :]
        await_bytes(hub_z_in.at[pl.ds(0, 3)], g_z[0])
        await_bytes(hub_z_sum, g_last[0])

    @pl.when(jnp.logical_not(holds))
    def _():
        await_bytes(hub_last, g_last[1])
        hub_row[...] = hub_last[pl.ds(pl.multiple_of(core * 8, 8), 8), :]
        await_bytes(hub_z_in.at[pl.ds(0, 4)], g_z[0])

    hub_mask = own_id == hub_at[0]
    for j in range(8):
        cols = slice(j * 128, (j + 1) * 128)
        own_sum[:, cols] += jnp.where(hub_mask, hub_row[j : j + 1, :], 0.0)

    from_y, rows = received(g2, ends_b)
    for n in range(4):
        own_sum[:, block(n)] += dot(picks[from_y], rows(n))
    from_y, rows = received(g3, ends_b)
    for n in range(4):
        grad[:, block(n)] = (own_sum[:, block(n)] + dot(picks[from_y], rows(n))).astype(BF16)
    for wait in sent:
        wait()


def tiles(count):
    return pltpu.VMEM((count, 16, 128), BF16)


ENDS = [
    tiles(128),
    tiles(128),
    pltpu.VMEM((4, X, 16, 16, 128), BF16),
    pltpu.VMEM((4, X - 1, 16, 16, 128), BF16),
    pltpu.VMEM((Y, X, Z, 16, 128), BF16),
]

SCRATCH = [
    pltpu.VMEM((NODES, WIDTH), BF16),
    pltpu.VMEM((NODES, WIDTH), BF16),
    pltpu.VMEM((32, WIDTH), BF16),
    pltpu.VMEM((16, NODES), I32),
    pltpu.VMEM((1, NODES), I32),
    pltpu.VMEM((1, BOUND), I32),
    pltpu.VMEM((BOUND, NODES), F32),
    pltpu.VMEM((X, NODES, 128), BF16),
    pltpu.VMEM((4096, 128), F32),
    pltpu.VMEM((1024, 128), F32),
    pltpu.VMEM((X, Z, 2, 16, WIDTH), BF16),
    pltpu.VMEM((NODES, COLUMNS), BF16),
    pltpu.VMEM((COLUMNS, NODES), BF16),
    pltpu.VMEM((HUBS, WIDTH), BF16),
    pltpu.VMEM((128, 128), F32),
    pltpu.VMEM((NODES, WIDTH), F32),
    pltpu.VMEM((NODES, WIDTH), BF16),
    pltpu.VMEM((NODES, WIDTH), BF16),
    pltpu.VMEM((NODES, WIDTH), F32),
    pltpu.VMEM((NODES, WIDTH), BF16),
    pltpu.VMEM((NODES, WIDTH), BF16),
    pltpu.VMEM((NODES, WIDTH), F32),
    *ENDS,
    *ENDS,
    pltpu.VMEM((16, 128), BF16),
    pltpu.VMEM((16, 128), BF16),
    tiles(256),
    pltpu.VMEM((4096, 128), F32),
    pltpu.VMEM((X, 512, 128), F32),
    pltpu.VMEM((X - 1, 512, 128), BF16),
    pltpu.VMEM((X - 1, 512, 128), BF16),
    pltpu.VMEM((512, 128), F32),
    pltpu.VMEM((Y, 64, 128), BF16),
    pltpu.VMEM((Y - 1, 64, 128), BF16),
    pltpu.VMEM((64, 128), F32),
    pltpu.VMEM((Z - 1, 16, 128), F32),
    pltpu.VMEM((16, 128), F32),
    pltpu.VMEM((16, 128), F32),
    pltpu.VMEM((8, 128), F32),
    pltpu.SemaphoreType.DMA((48,)),
    pltpu.SemaphoreType.DMA((48,)),
    pltpu.SemaphoreType.DMA((6,)),
    pltpu.SemaphoreType.REGULAR((Y,)),
]


def on_device(feat, cotangent, weight, nbr_index, degree, send_rows, hub_rows):
    vmem = pl.BlockSpec(memory_space=pltpu.VMEM)
    hbm = pl.BlockSpec(memory_space=pltpu.HBM)
    smem = pl.BlockSpec(memory_space=pltpu.SMEM)
    return pl.pallas_call(
        whole_kernel,
        out_shape=(
            jax.ShapeDtypeStruct((NODES, WIDTH), BF16),
            jax.ShapeDtypeStruct((NODES, WIDTH), BF16),
        ),
        in_specs=[hbm] * 6 + [smem],
        out_specs=(vmem, vmem),
        scratch_shapes=SCRATCH,
        compiler_params=pltpu.CompilerParams(has_side_effects=True, collective_id=0, vmem_limit_bytes=63 << 20),
        name="sage",
    )(feat, cotangent, weight, nbr_index.T, degree[None, :], send_rows.T, hub_rows)


def solution(mesh):
    placed = (
        P(("region", "sub"), None),
        P(("region", "sub"), None),
        P("sub", None),
        P(("region", "sub"), None),
        P(("region", "sub")),
        P(("region", "sub"), None),
        P(("region", "sub")),
    )
    return jax.shard_map(
        on_device,
        mesh=mesh,
        in_specs=placed,
        out_specs=(P(("region", "sub"), None), P(("region", "sub"), None)),
        check_vma=False,
    )
```

```python
import jax
import jax.numpy as jnp
from jax import lax
from jax.experimental import pallas as pl
from jax.experimental.pallas import tpu as pltpu
from jax.sharding import PartitionSpec as P

MESH = pl.DeviceIdType.MESH
BF16, F32, I32 = jnp.bfloat16, jnp.float32, jnp.int32
Y, X, Z = 8, 4, 8
NODES, WIDTH, BOUND, HUBS = 128, 1024, 512, 512
COLUMNS = NODES + BOUND + HUBS
GROUPS = (2, 1, 3, 0)


def place():
    region = lax.axis_index("region")
    sub = lax.axis_index("sub")
    return region // 2, region % 2, sub // 8, sub % 8


def device(y, core, x, z):
    return (y * 2 + core, x * 8 + z)


def remote(src, dst, sems, target):
    pltpu.make_async_remote_copy(
        src_ref=src, dst_ref=dst, send_sem=sems[0], recv_sem=sems[1], device_id=target, device_id_type=MESH
    ).start()


def await_bytes(ref, sem):
    pltpu.make_async_copy(ref, ref, sem).wait()


def dot(a, b):
    return jnp.dot(a, b, preferred_element_type=F32)


def block(n):
    return slice(n * 256, (n + 1) * 256)


def whole_kernel(
    feat_hbm, cot_hbm, shard_hbm, nbr_hbm, degree_hbm, send_hbm, hub_at,
    out, grad,
    feat, cot, shard, nbr_t, degree, send_row,
    pick_rows, picks, table, wide, full_weight, edges, edges_t, hub_lookup, div, total, mean, act, terms, high, low, own_sum,
    swap_out_f, swap_in_f, stage_f, mid_f, came_f, swap_out_b, swap_in_b, stage_b, mid_b, came_b,
    hub_tile, hub_other, hub_tiles, hub_table,
    hub_core, hub_x_out, hub_x_in, hub_x_sum, hub_y_out, hub_y_in, hub_y_sum, hub_z_in, hub_z_sum, hub_last, hub_row,
    send_sems, recv_sems, load_sems, entered,
):
    y, core, x, z = place()
    slot_y = (y % 4) * 2 + y // 4
    partner = device(y, 1 - core, x, z)
    holds = core == z // 4
    sem_ids = iter(range(64))
    due = {}
    sent = []

    def sems():
        i = next(sem_ids)
        return send_sems.at[i], recv_sems.at[i]

    def expect(name, ref, sem):
        due[name] = lambda: await_bytes(ref, sem)

    def settle(name):
        due.pop(name)()

    def leaves(ref, sem):
        sent.append(lambda: await_bytes(ref, sem))

    barrier = pltpu.get_barrier_semaphore()
    y_line = [device((y + d) % 8, core, x, z) for d in range(1, Y)]
    z_line = [device(y, core, x, (z + d) % 8) for d in range(1, Z)]
    x_line = [device(y, core, (x + d) % 4, z) for d in range(1, X)]
    for other in [partner] + x_line + y_line + z_line:
        pl.semaphore_signal(barrier, inc=1, device_id=other, device_id_type=MESH)

    loads = []
    for i, (src, dst) in enumerate(
        zip((send_hbm, feat_hbm, shard_hbm, nbr_hbm, degree_hbm, cot_hbm), (send_row, feat, shard, nbr_t, degree, cot))
    ):
        loads.append(pltpu.make_async_copy(src, dst, load_sems.at[i]))
        loads[i].start()

    loads[0].wait()
    own_id = lax.broadcasted_iota(I32, (NODES, 128), 0)
    for b in range(BOUND // 128):
        one_hot = jnp.where(own_id == send_row[:, b * 128 : (b + 1) * 128], 1.0, 0.0)
        pick_rows[b * 128 : (b + 1) * 128, :] = one_hot.T
    hub_pick = jnp.where(lax.broadcasted_iota(I32, (16, NODES), 1) == hub_at[0], 1.0, 0.0).astype(BF16)
    loads[1].wait()
    hub_wide = dot(hub_pick, feat[...])[0:8]
    lane_group = lax.broadcasted_iota(I32, (8, 128), 0)
    own_hub = jnp.zeros((8, 128), F32)
    for j in range(8):
        own_hub = jnp.where(lane_group == j, hub_wide[:, j * 128 : (j + 1) * 128], own_hub)
    hub_tile[...] = jnp.concatenate([own_hub, own_hub], axis=0).astype(BF16)
    def in_tiles(ref, base, n, part):
        for e in range(2):
            ref[pl.ds(base + 2 * n + e, part.shape[0], stride=8), :] = part[:, e * 128 : (e + 1) * 128]

    def table_row(g, dx, i, which):
        row = ((y + g + i // 8 * 4) % 8) * 64 + which * 32 + (4 - dx) % 4 * 8 + (z + i) % 8
        return table[pl.ds(pl.multiple_of(row * 8, 8), 8), :]

    def swap_build(g, ends):
        swap_out = ends["swap_out"]
        for dx in range(X):

            def build(m, carry):
                rows = [table_row(g, dx, 2 * m + e, 1) for e in range(2)]
                swap_out[g * 32 + dx * 8 + m] = jnp.concatenate(rows, axis=0).astype(BF16)
                return carry

            lax.fori_loop(0, 8, build, 0, unroll=4)

    def swap_send(g, ends):
        swap_out, swap_in, pair = ends["swap_out"], ends["swap_in"], ends["swap"][g]
        part = pl.ds(g * 32, 32)
        remote(swap_out.at[part], swap_in.at[part], pair, partner)
        expect(("swap", g), swap_in.at[part], pair[1])
        leaves(swap_out.at[part], pair[0])

    def along_x(g, ends):
        stage, mid = ends["stage"], ends["mid"]
        settle(("swap", g))
        for dx in (2, 1, 3, 0):

            def pair_up(m, carry):
                theirs = ends["swap_in"][g * 32 + dx * 8 + m].astype(F32)
                for e in range(2):
                    i = 2 * m + e
                    tile = jnp.concatenate([table_row(g, dx, i, 0), theirs[8 * e : 8 * e + 8]], axis=0)
                    stage[g, dx, i] = tile.astype(BF16)
                return carry

            lax.fori_loop(0, 8, pair_up, 0, unroll=4)
            if dx:
                remote(stage.at[g, dx], mid.at[g, dx - 1], ends["x"][g], x_line[dx - 1])
        expect(("x", g), mid.at[g], ends["x"][g][1])
        leaves(mid.at[g], ends["x"][g][0])

    def to_plane(g, ends, name, src, dst, tile_count):
        pair = ends[name][g]

        def post(i, carry):
            to = device((y + g + i // 8 * 4) % 8, core, x, (z + i) % 8)
            remote(src(i), dst, pair, to)
            return carry

        first = 0 if g else 1
        lax.fori_loop(first, 16, post, 0)
        same_size = tile_count(16 - first)
        expect((name, g), same_size, pair[1])
        leaves(same_size, pair[0])

    def post_own(g, ends):
        stage, came = ends["stage"], ends["came"]
        to_plane(
            g, ends, "own", lambda i: stage.at[g, 0, i], came.at[slot_y, 0, z], lambda n: stage.at[g, 0, pl.ds(0, n)]
        )
        if g == 0:
            came[slot_y, 0, z] = stage[0, 0, 0]

    def post_far(g, ends):
        mid, came = ends["mid"], ends["came"]
        settle(("x", g))
        to_plane(
            g, ends, "far", lambda i: mid.at[g, :, i], came.at[slot_y, pl.ds(1, 3), z], lambda n: mid.at[g, :, pl.ds(0, n)]
        )
        if g == 0:
            for d in range(3):
                came[slot_y, 1 + d, z] = mid[0, d, 0]

    def received(g, ends):
        came = ends["came"]
        settle(("own", g))
        settle(("far", g))
        from_y = (y + 4 - g) % 4
        for h in range(2):
            wide[h * 512 : (h + 1) * 512, :] = came[from_y * 2 + h].reshape(512, 128).astype(F32)

        def columns(n):
            sides = []
            for j in (2 * n, 2 * n + 1):
                parts = [wide[pl.ds(h * 512 + w * 8 + j, 32, stride=16), :] for h in range(2) for w in range(2)]
                sides.append(jnp.concatenate(parts, axis=0))
            return jnp.concatenate(sides, axis=1).astype(BF16)

        return from_y, columns

    def exchange_ends(swap_out, swap_in, stage, mid, came):
        ends = dict(swap_out=swap_out, swap_in=swap_in, stage=stage, mid=mid, came=came)
        for name in ("swap", "x", "own", "far"):
            ends[name] = [sems() for _ in GROUPS]
        return ends

    def to_table(base_y, n, part):
        for h in range(2):
            in_tiles(table, (h * 4 + base_y) * 512, n, part[h * 64 : (h + 1) * 64])

    ends_f = exchange_ends(swap_out_f, swap_in_f, stage_f, mid_f, came_f)

    def select(g):
        to_y = (y + g) % 4
        rows = []
        for h in range(2):
            for which in range(2):
                other = (core + which) % 2
                for q in range(X):
                    row = (h * 4 + to_y) * 64 + other * 32 + (x + 4 - q) % 4 * 8
                    rows.append(pick_rows[pl.ds(pl.multiple_of(row, 8), 8), :])
        chosen = jnp.concatenate(rows, axis=0)
        picks[to_y] = chosen.T.astype(BF16)
        chosen = chosen.astype(BF16)
        for n in range(4):
            to_table(to_y, n, dot(chosen, feat[:, block(n)]))

    g0, g1, g2, g3 = GROUPS
    select(g0)
    swap_build(g0, ends_f)
    select(g1)
    loads[2].wait()
    pl.semaphore_wait(barrier, len(x_line) + len(y_line) + len(z_line) + 1)
    for d in range(1, Y):
        pl.semaphore_signal(entered.at[Y - d], inc=1, device_id=y_line[d - 1], device_id_type=MESH)
    swap_send(g0, ends_f)

    w_z, w_x, w_core = sems(), sems(), sems()
    half = pl.ds(pl.multiple_of(core * 16, 16), 16)
    for other in z_line:
        remote(shard.at[half], full_weight.at[x, z, core], w_z, other)
    expect("w_z", full_weight.at[0, pl.ds(0, 7), 0], w_z[1])
    leaves(full_weight.at[0, pl.ds(0, 7), 0], w_z[0])
    h_core, h_z, h_y, h_x, h_last = sems(), sems(), sems(), sems(), sems()
    remote(hub_tile, hub_other, h_core, partner)
    expect("h_core", hub_other, h_core[1])
    leaves(hub_tile, h_core[0])
    full_weight[x, z, 0] = shard[0:16]
    full_weight[x, z, 1] = shard[16:32]

    settle("h_core")
    theirs = hub_other[...].astype(F32)[0:8]
    first = jnp.where(core == 0, own_hub, theirs)
    second = jnp.where(core == 0, theirs, own_hub)
    z_slab = ((x * 2 + core) * 8 + y) * 4

    @pl.when(holds)
    def _():
        slot = z_slab + z % 4
        hub_tiles[slot] = jnp.concatenate([first, second], axis=0).astype(BF16)
        for other in z_line:
            remote(hub_tiles.at[slot], hub_tiles.at[slot], h_z, other)

    def hub_z_due():
        @pl.when(holds)
        def _():
            await_bytes(hub_tiles.at[pl.ds(0, 3)], h_z[1])

        @pl.when(jnp.logical_not(holds))
        def _():
            await_bytes(hub_tiles.at[pl.ds(0, 4)], h_z[1])

    def hub_z_left():
        @pl.when(holds)
        def _():
            await_bytes(hub_tiles.at[pl.ds(0, 7)], h_z[0])

    due["h_z"] = hub_z_due
    sent.append(hub_z_left)
    along_x(g0, ends_f)
    swap_build(g1, ends_f)
    swap_send(g1, ends_f)

    def greeted(g):
        for dy in (g, g + 4):
            if dy:
                pl.semaphore_wait(entered.at[dy], 1)

    greeted(g0)
    post_own(g0, ends_f)
    select(g2)
    along_x(g1, ends_f)
    greeted(g1)
    post_own(g1, ends_f)
    swap_build(g2, ends_f)
    swap_send(g2, ends_f)
    select(g3)
    along_x(g2, ends_f)
    post_far(g0, ends_f)
    greeted(g2)
    post_own(g2, ends_f)
    swap_build(g3, ends_f)
    swap_send(g3, ends_f)

    settle("h_z")
    y_slab = pl.ds(z_slab, 4)
    for other in y_line:
        remote(hub_tiles.at[y_slab], hub_tiles.at[y_slab], h_y, other)
    expect("h_y", hub_tiles.at[pl.ds(0, 28)], h_y[1])
    leaves(hub_tiles.at[pl.ds(0, 28)], h_y[0])
    along_x(g3, ends_f)

    settle("w_z")
    for other in x_line:
        remote(full_weight.at[x, :, core], full_weight.at[x, :, core], w_x, other)
    expect("w_x", full_weight.at[pl.ds(0, 3), :, 0], w_x[1])
    leaves(full_weight.at[pl.ds(0, 3), :, 0], w_x[0])
    post_far(g1, ends_f)
    greeted(g3)
    post_own(g3, ends_f)
    post_far(g2, ends_f)

    settle("h_y")
    x_slab = pl.ds((x * 2 + core) * 32, 32)
    for other in x_line:
        remote(hub_tiles.at[x_slab], hub_tiles.at[x_slab], h_x, other)
    expect("h_x", hub_tiles.at[pl.ds(0, 96)], h_x[1])
    leaves(hub_tiles.at[pl.ds(0, 96)], h_x[0])
    post_far(g3, ends_f)

    loads[3].wait()
    loads[4].wait()
    number = nbr_t[...]
    s = number - NODES
    bound_column = (
        NODES + ((s >> 6) & 3) * 128 + (s >> 8) * 64 + (((s >> 5) + core) & 1) * 32
        + ((x - (s >> 3)) & 3) * 8 + (s & 7)
    )
    h = number - (NODES + BOUND)
    hub_column = (
        NODES + BOUND
        + ((((h >> 3) & 3) * 2 + ((h >> 2) & 1)) * 32 + (h >> 6) * 4 + (h & 3)) * 2
        + ((h >> 5) & 1)
    )
    column = jnp.where(number < NODES, number, jnp.where(number < NODES + BOUND, bound_column, hub_column))
    slot_id = lax.broadcasted_iota(I32, number.shape, 0)
    live = jnp.where(slot_id < degree[...], column, -1)
    for b in range(COLUMNS // 128):
        row_id = own_id + b * 128
        count = jnp.zeros((128, 128), F32)
        for k in range(live.shape[0]):
            count = count + jnp.where(live[k : k + 1, :] == row_id, 1.0, 0.0)
        edges_t[b * 128 : (b + 1) * 128, :] = count.astype(BF16)
        edges[:, b * 128 : (b + 1) * 128] = count.T.astype(BF16)
    div[...] = jnp.broadcast_to((degree[...] + 1).astype(F32), (128, 128)).T
    for n in range(4):
        rows = feat[:, block(n)]
        total[:, block(n)] = rows.astype(F32) + dot(edges[:, 0:NODES], rows)

    settle("h_x")
    for at in range(X):
        slab = pl.ds((at * 2 + core) * 32, 32)
        remote(hub_tiles.at[slab], hub_tiles.at[slab], h_last, partner)
    expect("h_last", hub_tiles.at[pl.ds(0, 128)], h_last[1])
    leaves(hub_tiles.at[pl.ds(0, 128)], h_last[0])
    settle("w_x")
    remote(full_weight.at[:, :, core], full_weight.at[:, :, core], w_core, partner)
    expect("w_core", full_weight.at[:, :, 0], w_core[1])
    leaves(full_weight.at[:, :, 0], w_core[0])

    settle("h_last")
    for part in range(8):
        hub_table[part * 512 : (part + 1) * 512, :] = (
            hub_tiles[part * 32 : (part + 1) * 32].reshape(512, 128).astype(F32)
        )
    for j in range(8):
        hub_lookup[:, j * 128 : (j + 1) * 128] = hub_table[pl.ds(j, HUBS, stride=8), :].astype(BF16)
    for n in range(4):
        total[:, block(n)] += dot(edges[:, NODES + BOUND : COLUMNS], hub_lookup[:, block(n)])

    for g in GROUPS:
        from_y, rows = received(g, ends_f)
        part = edges[:, pl.ds(pl.multiple_of(NODES + from_y * 128, 128), 128)]
        for n in range(4):
            total[:, block(n)] += dot(part, rows(n))

    settle("w_core")
    loads[5].wait()
    two_div = jnp.concatenate([div[...], div[...]], axis=1)
    for n in range(4):
        mean[:, block(n)] = (total[:, block(n)] / two_div).astype(BF16)
    for n in range(4):
        pre_act = jnp.zeros((NODES, 256), F32)
        for k in range(X):
            pre_act = pre_act + dot(mean[:, block(k)], full_weight[k, :, :, :, block(n)].reshape(256, 256))
        sig = jax.nn.sigmoid(pre_act)
        out[:, block(n)] = (pre_act * sig).astype(BF16)
        slope = sig * (1.0 + pre_act * (1.0 - sig))
        act[:, block(n)] = (cot[:, block(n)].astype(F32) * slope).astype(BF16)
    for n in range(X):
        term = lax.dot_general(
            act[...], full_weight[n].reshape(256, WIDTH), (((1,), (1,)), ((), ())), preferred_element_type=F32
        ) / two_div
        top = term.astype(BF16)
        terms[:, block(n)] = term
        high[:, block(n)] = top
        low[:, block(n)] = (term - top.astype(F32)).astype(BF16)

    def spread(rows, put):
        edge = edges_t[rows, :]
        for n in range(4):
            put(n, dot(edge, high[:, block(n)]) + dot(edge, low[:, block(n)]))

    ends_b = exchange_ends(swap_out_b, swap_in_b, stage_b, mid_b, came_b)
    g_core, g_x, g_y, g_z, g_last = sems(), sems(), sems(), sems(), sems()

    def give_back(g):
        to_y = (y + g) % 4
        spread(
            pl.ds(pl.multiple_of(NODES + to_y * 128, 128), 128), lambda n, part: to_table(to_y, n, part)
        )
        swap_build(g, ends_b)
        swap_send(g, ends_b)

    give_back(g0)

    give_back(g1)
    along_x(g0, ends_b)
    post_own(g0, ends_b)

    spread(slice(NODES + BOUND, COLUMNS), lambda n, part: in_tiles(hub_table, 0, n, part))
    for at in range(X):
        slab = pl.ds(pl.multiple_of((at * 2 + 1 - core) * 512, 512), 512)
        remote(hub_table.at[slab], hub_core.at[at], g_core, partner)
    expect("g_core", hub_core, g_core[1])
    leaves(hub_core, g_core[0])
    along_x(g1, ends_b)
    post_own(g1, ends_b)
    give_back(g2)

    def kept(at):
        return hub_table[pl.ds(pl.multiple_of((at * 2 + core) * 512, 512), 512), :] + hub_core[at]

    settle("g_core")
    for d in range(1, X):
        hub_x_out[d - 1] = kept((x + d) % 4).astype(BF16)
        remote(hub_x_out.at[d - 1], hub_x_in.at[d - 1], g_x, x_line[d - 1])
    expect("g_x", hub_x_in, g_x[1])
    leaves(hub_x_in, g_x[0])
    post_far(g0, ends_b)
    along_x(g2, ends_b)
    post_own(g2, ends_b)
    give_back(g3)
    post_far(g1, ends_b)
    along_x(g3, ends_b)
    post_own(g3, ends_b)

    settle("g_x")
    part = kept(x)
    for d in range(X - 1):
        part = part + hub_x_in[d].astype(F32)
    hub_x_sum[...] = part
    hub_y_out[...] = part.astype(BF16).reshape(Y, 64, 128)
    for d in range(1, Y):
        remote(hub_y_out.at[(y + d) % 8], hub_y_in.at[d - 1], g_y, y_line[d - 1])
    expect("g_y", hub_y_in, g_y[1])
    leaves(hub_y_in, g_y[0])
    post_far(g2, ends_b)
    post_far(g3, ends_b)

    for n in range(4):
        cols = block(n)
        own_sum[:, cols] = terms[:, cols] + dot(edges_t[0:NODES, :], high[:, cols]) + dot(edges_t[0:NODES, :], low[:, cols])
    settle("g_y")
    part = hub_x_sum[pl.ds(pl.multiple_of(y * 64, 64), 64), :]
    for d in range(Y - 1):
        part = part + hub_y_in[d].astype(F32)
    hub_y_sum[...] = part
    for at in range(4):
        to = core * 4 + at

        @pl.when(to != z)
        def _():
            slot = (to - z + 8) % 8 - 1
            remote(hub_y_sum.at[pl.ds(at * 16, 16)], hub_z_in.at[slot], g_z, device(y, core, x, to))

    for g in (g0, g1):
        from_y, rows = received(g, ends_b)
        for n in range(4):
            own_sum[:, block(n)] += dot(picks[from_y], rows(n))

    @pl.when(holds)
    def _():
        await_bytes(hub_z_in, g_z[1])
        here = hub_y_sum[pl.ds(pl.multiple_of((z % 4) * 16, 16), 16), :]
        for d in range(Z - 1):
            here = here + hub_z_in[d]
        hub_z_sum[...] = here
        remote(hub_z_sum, hub_last, g_last, partner)
        hub_row[...] = hub_z_sum[pl.ds(pl.multiple_of(core * 8, 8), 8), :]
        await_bytes(hub_z_in.at[pl.ds(0, 3)], g_z[0])
        await_bytes(hub_z_sum, g_last[0])

    @pl.when(jnp.logical_not(holds))
    def _():
        await_bytes(hub_last, g_last[1])
        hub_row[...] = hub_last[pl.ds(pl.multiple_of(core * 8, 8), 8), :]
        await_bytes(hub_z_in.at[pl.ds(0, 4)], g_z[0])

    hub_mask = own_id == hub_at[0]
    for j in range(8):
        cols = slice(j * 128, (j + 1) * 128)
        own_sum[:, cols] += jnp.where(hub_mask, hub_row[j : j + 1, :], 0.0)

    from_y, rows = received(g2, ends_b)
    for n in range(4):
        own_sum[:, block(n)] += dot(picks[from_y], rows(n))
    from_y, rows = received(g3, ends_b)
    for n in range(4):
        grad[:, block(n)] = (own_sum[:, block(n)] + dot(picks[from_y], rows(n))).astype(BF16)
    for wait in sent:
        wait()


def tiles(count):
    return pltpu.VMEM((count, 16, 128), BF16)


ENDS = [
    tiles(128),
    tiles(128),
    pltpu.VMEM((4, X, 16, 16, 128), BF16),
    pltpu.VMEM((4, X - 1, 16, 16, 128), BF16),
    pltpu.VMEM((Y, X, Z, 16, 128), BF16),
]

SCRATCH = [
    pltpu.VMEM((NODES, WIDTH), BF16),
    pltpu.VMEM((NODES, WIDTH), BF16),
    pltpu.VMEM((32, WIDTH), BF16),
    pltpu.VMEM((16, NODES), I32),
    pltpu.VMEM((1, NODES), I32),
    pltpu.VMEM((1, BOUND), I32),
    pltpu.VMEM((BOUND, NODES), F32),
    pltpu.VMEM((X, NODES, 128), BF16),
    pltpu.VMEM((4104, 128), F32),
    pltpu.VMEM((1040, 128), F32),
    pltpu.VMEM((X, Z, 2, 16, WIDTH), BF16),
    pltpu.VMEM((NODES, COLUMNS), BF16),
    pltpu.VMEM((COLUMNS, NODES), BF16),
    pltpu.VMEM((HUBS, WIDTH), BF16),
    pltpu.VMEM((128, 128), F32),
    pltpu.VMEM((NODES, WIDTH), F32),
    pltpu.VMEM((NODES, WIDTH), BF16),
    pltpu.VMEM((NODES, WIDTH), BF16),
    pltpu.VMEM((NODES, WIDTH), F32),
    pltpu.VMEM((NODES, WIDTH), BF16),
    pltpu.VMEM((NODES, WIDTH), BF16),
    pltpu.VMEM((NODES, WIDTH), F32),
    *ENDS,
    *ENDS,
    pltpu.VMEM((16, 128), BF16),
    pltpu.VMEM((16, 128), BF16),
    tiles(256),
    pltpu.VMEM((4104, 128), F32),
    pltpu.VMEM((X, 512, 128), F32),
    pltpu.VMEM((X - 1, 512, 128), BF16),
    pltpu.VMEM((X - 1, 512, 128), BF16),
    pltpu.VMEM((512, 128), F32),
    pltpu.VMEM((Y, 64, 128), BF16),
    pltpu.VMEM((Y - 1, 64, 128), BF16),
    pltpu.VMEM((64, 128), F32),
    pltpu.VMEM((Z - 1, 16, 128), F32),
    pltpu.VMEM((16, 128), F32),
    pltpu.VMEM((16, 128), F32),
    pltpu.VMEM((8, 128), F32),
    pltpu.SemaphoreType.DMA((48,)),
    pltpu.SemaphoreType.DMA((48,)),
    pltpu.SemaphoreType.DMA((6,)),
    pltpu.SemaphoreType.REGULAR((Y,)),
]


def on_device(feat, cotangent, weight, nbr_index, degree, send_rows, hub_rows):
    vmem = pl.BlockSpec(memory_space=pltpu.VMEM)
    hbm = pl.BlockSpec(memory_space=pltpu.HBM)
    smem = pl.BlockSpec(memory_space=pltpu.SMEM)
    return pl.pallas_call(
        whole_kernel,
        out_shape=(
            jax.ShapeDtypeStruct((NODES, WIDTH), BF16),
            jax.ShapeDtypeStruct((NODES, WIDTH), BF16),
        ),
        in_specs=[hbm] * 6 + [smem],
        out_specs=(vmem, vmem),
        scratch_shapes=SCRATCH,
        compiler_params=pltpu.CompilerParams(has_side_effects=True, collective_id=0, vmem_limit_bytes=63 << 20),
        name="sage",
    )(feat, cotangent, weight, nbr_index.T, degree[None, :], send_rows.T, hub_rows)


def solution(mesh):
    placed = (
        P(("region", "sub"), None),
        P(("region", "sub"), None),
        P("sub", None),
        P(("region", "sub"), None),
        P(("region", "sub")),
        P(("region", "sub"), None),
        P(("region", "sub")),
    )
    return jax.shard_map(
        on_device,
        mesh=mesh,
        in_specs=placed,
        out_specs=(P(("region", "sub"), None), P(("region", "sub"), None)),
        check_vma=False,
    )
```
